32 devices in a mesh: farm: 2 (over x), body: 16 (over z, y, core).
Axes of the slice: x: 2, y: 2, z: 4, core: 2. Of those that a mesh axis runs over, the one named last changes fastest.
Arguments:
- incident: float32 [32, 2, 16, 768], P(('farm', 'body')), parts along dimension 0, may hold values from -6 to 6
- self_inverse: float32 [32, 2, 768, 768], P(('farm', 'body')), parts along dimension 0
- cross_blocks: float32 [32, 4, 2, 768, 768], P(('farm', 'body')), parts along dimension 0, may hold values from -0.046875 to 0.046875
- neighbours: int32 [32, 4], P(('farm', 'body')), parts along dimension 0, may hold values from -1 to 15, as said below
- panel_weight: float32 [32, 768], P(('farm', 'body')), parts along dimension 0, may hold values from -0.0546875 to 0.0546875
Outputs:
- sources: float32 [32, 2, 16, 768], P(('farm', 'body')), parts along dimension 0
- farm_force: float32 [2, 2, 16], P('farm'), parts along dimension 0
The draws below stay inside these ranges and needn't reach their ends.
There are 2 independent parts, one for each index of `farm`. The reference program is written for one: setup_inputs(seed, part) draws one part's arguments, and reference() takes and returns one part's arrays. A program takes and returns all parts, laid end to end along the dimension named above; each array names one. Nothing has to cross between parts.
Inputs may be any that keep to these rules, and one draw needn't show every extreme that they name: `neighbours`: each row names distinct bodies other than its own, each within 8 positions of it around the closed loop of 16 bodies; some body names the body exactly 8 positions away.
All inputs are finite; a program needn't handle non-finite values.
Results may differ from the reference program's by a relative error of at most 0.0003.
Values sent between devices are 32-bit elements; how exact they have to be, the bound alone decides.
No kernel may reach another device: no remote copies, remote signals or barrier semaphores. Data moves between devices by JAX's collectives and lax.ppermute only.
A program may use at most 128 MiB of HBM per device.

```python
import math
import jax
import jax.numpy as jnp
from jax import lax

PANELS = 768
HEADINGS = 16
SLOTS = 4
ITERS = 6
BODIES = 16
REACH = 8


def draw_self_inverse(key, part):
    key_off, key_diag = jax.random.split(jax.random.fold_in(key, 11))
    shape = (BODIES, 2, PANELS, PANELS)
    off = jax.random.normal(key_off, shape, jnp.float32) * (0.3 / math.sqrt(PANELS))
    diag = jax.random.uniform(key_diag, (BODIES, PANELS), jnp.float32, 0.5, 1.5)
    eye = jnp.arange(PANELS)[:, None] == jnp.arange(PANELS)[None, :]
    real_part = off[:, 0] + jnp.where(eye[None], diag[:, :, None], 0.0)
    return jnp.stack([real_part, off[:, 1]], axis=1).astype(jnp.float32)


def draw_neighbours(key, part):
    key_score, key_row, key_keep = jax.random.split(jax.random.fold_in(key, 23), 3)
    steps_up = jnp.arange(1, REACH + 1, dtype=jnp.int32)
    steps_down = -jnp.arange(1, REACH, dtype=jnp.int32)
    candidates = jnp.concatenate([steps_up, steps_down])
    width = 2 * REACH - 1
    scores = jax.random.randint(key_score, (BODIES, width), 0, 1 << 20) * width + jnp.arange(width, dtype=jnp.int32)[None]
    order = jnp.argsort(scores, axis=1, stable=True)[:, :SLOTS]
    offsets = candidates[order]
    special = jnp.array([REACH, 1, -1, 2], dtype=jnp.int32)[:SLOTS]
    chosen = jax.random.randint(key_row, (), 0, BODIES)
    is_chosen = (jnp.arange(BODIES) == chosen)[:, None]
    offsets = jnp.where(is_chosen, special[None], offsets)
    keep = (jax.random.randint(key_keep, (BODIES, SLOTS), 0, 4) > 0) | is_chosen
    source_index = (jnp.arange(BODIES, dtype=jnp.int32)[:, None] + offsets) % BODIES
    return jnp.where(keep, source_index, -1).astype(jnp.int32)


def block_levels(own_key, shape, shards, low, high):
    loudness = 1.0
    for axis_at, parts in shards:
        steps = jax.random.uniform(jax.random.fold_in(jax.random.fold_in(own_key, 6), axis_at), (parts,), jnp.float32, low / len(shards), high / len(shards))
        loudness = loudness * jnp.repeat(jnp.exp(steps), shape[axis_at] // parts).reshape((-1,) + (1,) * (len(shape) - 1 - axis_at))
    return loudness


def centred(rng, shape, deviation, bound, cuts=(), held_as=jnp.bfloat16):
    level = block_levels(rng, shape, cuts, -0.22, 0.18) if cuts else 1.0
    values = jax.random.normal(rng, shape, jnp.float32) * deviation * level
    return jnp.minimum(jnp.maximum(values, -bound), bound).astype(held_as)


def setup_inputs(seed: int = 0, part: int = 0) -> dict:
    keys = jax.random.split(jax.random.key(seed), 6)
    own_keys = jax.random.split(jax.random.fold_in(keys[5], part), 6)
    incident = centred(own_keys[0], (BODIES, 2, HEADINGS, PANELS), 1.0, 6.0, ((0, 16),), jnp.float32)
    self_inverse = draw_self_inverse(jax.random.fold_in(jax.random.fold_in(keys[5], part), 71), part)
    cross_blocks = centred(own_keys[2], (BODIES, SLOTS, 2, PANELS, PANELS), (25 * PANELS) ** -0.5, 0.046875, ((0, 16),), jnp.float32)
    neighbours = draw_neighbours(jax.random.fold_in(jax.random.fold_in(keys[5], part), 71), part)
    panel_weight = centred(own_keys[4], (BODIES, PANELS), (BODIES * PANELS) ** -0.5, 0.0546875, ((0, 16),), jnp.float32)
    return dict(incident=incident, self_inverse=self_inverse, cross_blocks=cross_blocks, neighbours=neighbours, panel_weight=panel_weight)


def complex_apply(matrix, field):
    heads = field.shape[1]
    stacked = field.reshape(2 * heads, field.shape[2])
    dims = (((1,), (1,)), ((), ()))
    real_part = lax.dot_general(stacked, matrix[0], dims, precision=lax.Precision.HIGHEST)
    imag_part = lax.dot_general(stacked, matrix[1], dims, precision=lax.Precision.HIGHEST)
    return jnp.stack([real_part[:heads] - imag_part[heads:], real_part[heads:] + imag_part[:heads]])


def reference(incident, self_inverse, cross_blocks, neighbours, panel_weight):
    live = neighbours >= 0
    safe = jnp.where(live, neighbours, 0).astype(jnp.int32)
    sources = lax.map(lambda pair: complex_apply(pair[0], pair[1]), (self_inverse, incident))
    for sweep in range(ITERS):
        previous = sources

        def update(items):
            inverse_one, blocks, field, index_row, flag_row = items
            total = field
            for slot in range(SLOTS):
                other = lax.dynamic_index_in_dim(previous, index_row[slot], 0, keepdims=False)
                total = total - jnp.where(flag_row[slot], complex_apply(blocks[slot], other), 0.0)
            return complex_apply(inverse_one, total)

        sources = lax.map(update, (self_inverse, cross_blocks, incident, safe, live))
    force = jnp.einsum("bp,bchp->ch", panel_weight, sources, precision=lax.Precision.HIGHEST)
    return sources, force[None]
```

```python
import functools

import jax
import jax.numpy as jnp
from jax import lax
from jax.experimental import pallas as pl
from jax.experimental.pallas import tpu as pltpu
from jax.sharding import PartitionSpec as P

ITERS = 6
NT = (((1,), (1,)), ((), ()))
TILE = 256


def split(x):
    hi = x.astype(jnp.bfloat16)
    lo = (x - hi.astype(jnp.float32)).astype(jnp.bfloat16)
    return hi, lo


def turn(x, heads):
    return jnp.concatenate([-x[heads:], x[:heads]], axis=0)


def put_field(lhs, slot, x, heads):
    hi, lo = split(x)
    hi, lo = hi.astype(jnp.float32), lo.astype(jnp.float32)
    lhs[2 * slot] = jnp.concatenate([hi, lo], axis=0).astype(jnp.bfloat16)
    lhs[2 * slot + 1] = jnp.concatenate(
        [turn(hi, heads), turn(lo, heads)], axis=0
    ).astype(jnp.bfloat16)


def product(lhs, hi_ref, lo_ref, count, store):
    rows = lhs.shape[1] // 2
    panels = lhs.shape[2]
    for start in range(0, panels, TILE):
        part = slice(start, start + TILE)
        both, low = None, None
        for j in range(count):
            a = lax.dot_general(lhs[j], hi_ref[j, part, :], NT, preferred_element_type=jnp.float32)
            b = lax.dot_general(lhs[j, :rows], lo_ref[j, part, :], NT, preferred_element_type=jnp.float32)
            both = a if both is None else both + a
            low = b if low is None else low + b
        store(part, both[:rows] + both[rows:] + low)


def split_kernel(m_ref, hi_ref, lo_ref):
    hi, lo = split(m_ref[0])
    j = pl.program_id(0)
    hi_ref[j] = hi
    lo_ref[j] = lo


def split_matrices(m):
    count, rows, cols = m.shape
    whole = pl.BlockSpec(m.shape, lambda j: (0, 0, 0))
    out = jax.ShapeDtypeStruct(m.shape, jnp.bfloat16)
    return pl.pallas_call(
        split_kernel,
        grid=(count,),
        in_specs=[pl.BlockSpec((1, rows, cols), lambda j: (j, 0, 0))],
        out_specs=[pl.BlockSpec(memory_space=pltpu.VMEM)] * 2,
        out_shape=[out, out],
        compiler_params=pltpu.CompilerParams(vmem_limit_bytes=12 * 2**20),
    )(m)


def first_kernel(heads, field_ref, hi_ref, lo_ref, out_ref, lhs):
    put_field(lhs, 0, field_ref[...], heads)

    def store(part, value):
        out_ref[:, part] = value

    product(lhs, hi_ref, lo_ref, 2, store)


def sweep_kernel(heads, slots, count, which_ref, *refs):
    blocks = refs[:count]
    field_ref, chi, clo, ihi, ilo, out_ref, near, lhs, load, sem = refs[count:]
    for k in range(slots):
        for j in range(count):
            @pl.when(which_ref[k] == j)
            def _():
                pltpu.make_async_copy(blocks[j], near.at[k], sem.at[k]).start()
    for k in range(slots):
        @pl.when(which_ref[k] >= 0)
        def _():
            pltpu.make_async_copy(blocks[0], near.at[k], sem.at[k]).wait()
            put_field(lhs, k, near[k], heads)

        @pl.when(which_ref[k] < 0)
        def _():
            put_field(lhs, k, jnp.zeros(near.shape[1:], jnp.float32), heads)

    def store_load(part, value):
        load[:, part] = field_ref[:, part] - value

    product(lhs, chi, clo, 2 * slots, store_load)
    put_field(lhs, 0, load[...], heads)

    def store(part, value):
        out_ref[:, part] = value

    product(lhs, ihi, ilo, 2, store)


def body(count, incident, self_inverse, cross_blocks, neighbours, panel_weight):
    _, _, heads, panels = incident.shape
    slots = cross_blocks.shape[1]
    rows = 2 * heads
    field = incident.reshape(rows, panels)
    me = lax.axis_index("body")
    lines = count // 4

    def rel(index):
        dz = lax.rem(me // 4 - index // 4 + lines, lines)
        return dz * 4 + jnp.bitwise_xor(lax.rem(index, 4), lax.rem(me, 4))

    row = neighbours[0]
    which = jnp.where(row >= 0, rel(jnp.maximum(row, 0)), -1)
    vmem = pl.BlockSpec(memory_space=pltpu.VMEM)
    out = jax.ShapeDtypeStruct((rows, panels), jnp.float32)
    small = pltpu.CompilerParams(vmem_limit_bytes=12 * 2**20)
    ihi, ilo = split_matrices(self_inverse[0])
    chi, clo = split_matrices(cross_blocks[0].reshape(2 * slots, panels, panels))
    sources = pl.pallas_call(
        functools.partial(first_kernel, heads),
        in_specs=[vmem] * 3,
        out_specs=vmem,
        out_shape=out,
        scratch_shapes=[pltpu.VMEM((2, 2 * rows, panels), jnp.bfloat16)],
        compiler_params=small,
    )(field, ihi, ilo)
    sweep_call = pl.pallas_call(
        functools.partial(sweep_kernel, heads, slots, count),
        in_specs=[pl.BlockSpec(memory_space=pltpu.SMEM)]
        + [pl.BlockSpec(memory_space=pl.ANY)] * count
        + [vmem] * 5,
        out_specs=vmem,
        out_shape=out,
        scratch_shapes=[
            pltpu.VMEM((slots, rows, panels), jnp.float32),
            pltpu.VMEM((2 * slots, 2 * rows, panels), jnp.bfloat16),
            pltpu.VMEM((rows, panels), jnp.float32),
            pltpu.SemaphoreType.DMA((slots,)),
        ],
        compiler_params=small,
    )

    def move(x, pairs):
        return lax.ppermute(x, "body", pairs)

    z_pairs = [[(i, (i + 4 * d) % count) for i in range(count)] for d in range(lines)]
    y_pairs = [(i, i ^ 2) for i in range(count)]
    c_pairs = [(i, i ^ 1) for i in range(count)]
    for sweep in range(ITERS):
        blocks = [None] * count
        for d in range(lines):
            blocks[4 * d] = sources if d == 0 else move(sources, z_pairs[d])
        for d in range(lines):
            blocks[4 * d + 2] = move(blocks[4 * d], y_pairs)
        for d in range(lines):
            blocks[4 * d + 1] = move(blocks[4 * d], c_pairs)
        for d in range(lines):
            blocks[4 * d + 3] = move(blocks[4 * d + 2], c_pairs)
        sources = sweep_call(which, *blocks, field, chi, clo, ihi, ilo)
    partial_force = jnp.sum(
        sources.reshape(2, heads, panels) * panel_weight[0][None, None], axis=-1
    )
    farm_force = lax.psum(partial_force, "body")
    return (sources.reshape(1, 2, heads, panels), farm_force[None])


def solution(mesh):
    return jax.shard_map(
        functools.partial(body, mesh.shape["body"]),
        mesh=mesh,
        in_specs=(
            P(("farm", "body"), None, None, None),
            P(("farm", "body"), None, None, None),
            P(("farm", "body"), None, None, None, None),
            P(("farm", "body"), None),
            P(("farm", "body"), None),
        ),
        out_specs=(P(("farm", "body"), None, None, None), P("farm", None, None)),
        check_vma=False,
    )
```

```python
import functools

import jax
import jax.numpy as jnp
from jax import lax
from jax.experimental import pallas as pl
from jax.experimental.pallas import tpu as pltpu
from jax.sharding import PartitionSpec as P

ITERS = 6
NT = (((1,), (1,)), ((), ()))
LIMIT = 14 * 2**20
VMEM = pl.BlockSpec(memory_space=pltpu.VMEM)
SMEM = pl.BlockSpec(memory_space=pltpu.SMEM)
HBM = pl.BlockSpec(memory_space=pltpu.HBM)


def split(x):
    hi = x.astype(jnp.bfloat16)
    lo = (x - hi.astype(jnp.float32)).astype(jnp.bfloat16)
    return hi, lo


def turn(x, heads):
    return jnp.concatenate([-x[heads:], x[:heads]], axis=0)


def split_all(src, wide, buffers, sems, chunk):
    count, rows, cols = src.shape
    half = count * cols
    steps = [(j, r) for j in range(count) for r in range(0, rows, chunk)]
    depth = buffers.shape[0]

    def copy(i):
        j, r = steps[i]
        return pltpu.make_async_copy(
            src.at[j, pl.ds(r, chunk)], buffers.at[i % depth], sems.at[i % depth]
        )

    for i in range(min(depth, len(steps))):
        copy(i).start()
    for i, (j, r) in enumerate(steps):
        copy(i).wait()
        hi, lo = split(buffers[i % depth])
        wide[r:r + chunk, j * cols:(j + 1) * cols] = hi
        wide[r:r + chunk, half + j * cols:half + (j + 1) * cols] = lo
        if i + depth < len(steps):
            copy(i + depth).start()


def put_field(lhs, slot, x, heads):
    rows, panels = x.shape
    half = lhs.shape[1] // 2
    hi, lo = split(x)
    hi, lo = hi.astype(jnp.float32), lo.astype(jnp.float32)
    for c in range(2):
        at = (2 * slot + c) * panels
        a = (turn(hi, heads) if c else hi).astype(jnp.bfloat16)
        b = (turn(lo, heads) if c else lo).astype(jnp.bfloat16)
        lhs[:rows, at:at + panels] = a
        lhs[rows:, at:at + panels] = b
        lhs[:rows, half + at:half + at + panels] = a
        lhs[rows:, half + at:half + at + panels] = jnp.zeros_like(b)


def product(wide, lhs, width, rows, step):
    total = None
    for at in range(0, width, step):
        term = lax.dot_general(
            wide[:, at:at + step], lhs[:, at:at + step], NT, preferred_element_type=jnp.float32
        )
        total = term if total is None else total + term
    flat = total.T
    return flat[:rows] + flat[rows:]


def first_kernel(heads, inverse, field_ref, wide, out_ref, lhs, buffers, sems):
    split_all(inverse, wide, buffers, sems, buffers.shape[1])
    put_field(lhs, 0, field_ref[...], heads)
    rows, panels = field_ref.shape
    out_ref[...] = product(wide, lhs, 4 * panels, rows, 2 * panels)


def split_kernel(src, field_ref, wide, same_ref, buffers, sems):
    split_all(src, wide, buffers, sems, buffers.shape[1])
    same_ref[...] = field_ref[...]


def sweep_kernel(heads, slots, count, last, which_ref, *refs):
    blocks = refs[:count]
    field_ref, cross, inverse = refs[count:count + 3]
    refs = refs[count + 3:]
    if last:
        weight_ref, out_ref, part_ref, near, lhs = refs
    else:
        out_ref, near, lhs = refs
    rows, panels = field_ref.shape
    for k in range(slots):
        for j in range(count):
            @pl.when(which_ref[k] == j)
            def _():
                near[...] = blocks[j][...]

        @pl.when(which_ref[k] < 0)
        def _():
            near[...] = jnp.zeros_like(near)

        put_field(lhs, k, near[...], heads)
    width = 4 * slots * panels
    load = field_ref[...] - product(cross, lhs, width, rows, 2 * panels)
    short = lhs.at[:, :4 * panels]
    put_field(short, 0, load, heads)
    value = product(inverse, short, 4 * panels, rows, 2 * panels)
    out_ref[...] = value
    if last:
        part = jnp.sum(value * weight_ref[...], axis=1, keepdims=True)
        part_ref[...] = jnp.broadcast_to(part, part_ref.shape)


def body(count, incident, self_inverse, cross_blocks, neighbours, panel_weight):
    _, _, heads, panels = incident.shape
    slots = cross_blocks.shape[1]
    rows = 2 * heads
    field = incident.reshape(rows, panels)
    me = lax.axis_index("body")
    lines = count // 4

    def rel(index):
        dz = lax.rem(me // 4 - index // 4 + lines, lines)
        return dz * 4 + jnp.bitwise_xor(lax.rem(index, 4), lax.rem(me, 4))

    row = neighbours[0]
    which = jnp.where(row >= 0, rel(jnp.maximum(row, 0)), -1)
    out = jax.ShapeDtypeStruct((rows, panels), jnp.float32)
    tiny = jax.ShapeDtypeStruct((rows, 128), jnp.float32)
    params = pltpu.CompilerParams(vmem_limit_bytes=LIMIT)
    chunk = panels // 2
    inverse, sources = pl.pallas_call(
        functools.partial(first_kernel, heads),
        in_specs=[HBM, VMEM],
        out_specs=[VMEM, VMEM],
        out_shape=[jax.ShapeDtypeStruct((panels, 4 * panels), jnp.bfloat16), out],
        scratch_shapes=[
            pltpu.VMEM((2 * rows, 4 * panels), jnp.bfloat16),
            pltpu.VMEM((4, chunk, panels), jnp.float32),
            pltpu.SemaphoreType.DMA((4,)),
        ],
        compiler_params=params,
    )(pltpu.with_memory_space_constraint(self_inverse[0], pltpu.HBM), field)
    size = cross_blocks.size * 4
    all_blocks = cross_blocks[0].reshape(2 * slots, panels, panels)
    cross, same = pl.pallas_call(
        split_kernel,
        in_specs=[HBM, VMEM],
        out_specs=[VMEM, VMEM],
        out_shape=[jax.ShapeDtypeStruct((panels, 4 * slots * panels), jnp.bfloat16), out],
        scratch_shapes=[
            pltpu.VMEM((6, chunk, panels), jnp.float32),
            pltpu.SemaphoreType.DMA((6,)),
        ],
        compiler_params=params,
        cost_estimate=pl.CostEstimate(flops=4 * size, bytes_accessed=size, transcendentals=0),
    )(pltpu.with_memory_space_constraint(all_blocks, pltpu.HBM), sources)

    def sweep(last, *args):
        return pl.pallas_call(
            functools.partial(sweep_kernel, heads, slots, count, last),
            in_specs=[SMEM] + [VMEM] * (len(args) - 1),
            out_specs=[VMEM, VMEM] if last else VMEM,
            out_shape=[out, tiny] if last else out,
            scratch_shapes=[
                pltpu.VMEM((rows, panels), jnp.float32),
                pltpu.VMEM((2 * rows, 4 * slots * panels), jnp.bfloat16),
            ],
            compiler_params=params,
        )(*args)

    def move(x, pairs):
        return lax.ppermute(x, "body", pairs)

    z_pairs = [[(i, (i + 4 * d) % count) for i in range(count)] for d in range(lines)]
    y_pairs = [(i, i ^ 2) for i in range(count)]
    c_pairs = [(i, i ^ 1) for i in range(count)]
    for step in range(ITERS):
        blocks = [None] * count
        own = sources if step else same
        for d in range(lines):
            blocks[4 * d] = sources if d == 0 else move(sources, z_pairs[d])
        for d in range(lines):
            blocks[4 * d + 2] = move(blocks[4 * d] if d else own, y_pairs)
        for d in range(lines):
            blocks[4 * d + 1] = move(blocks[4 * d] if d else own, c_pairs)
        for d in range(lines):
            blocks[4 * d + 3] = move(blocks[4 * d + 2], c_pairs)
        args = (which, *blocks, field, cross, inverse)
        if step == ITERS - 1:
            sources, part = sweep(True, *args, panel_weight)
        else:
            sources = sweep(False, *args)
    terms = [part] + [move(part, z_pairs[d]) for d in range(1, lines)]
    while len(terms) > 1:
        half = len(terms) // 2
        terms = [terms[i] + terms[i + half] for i in range(half)]
    part = terms[0]
    part = part + move(part, y_pairs)
    part = part + move(part, c_pairs)
    farm_force = part[:, 0].reshape(1, 2, heads)
    return (sources.reshape(1, 2, heads, panels), farm_force)


def solution(mesh):
    return jax.shard_map(
        functools.partial(body, mesh.shape["body"]),
        mesh=mesh,
        in_specs=(
            P(("farm", "body"), None, None, None),
            P(("farm", "body"), None, None, None),
            P(("farm", "body"), None, None, None, None),
            P(("farm", "body"), None),
            P(("farm", "body"), None),
        ),
        out_specs=(P(("farm", "body"), None, None, None), P("farm", None, None)),
        check_vma=False,
    )
```

```python
import functools

import jax
import jax.numpy as jnp
from jax import lax
from jax.experimental import pallas as pl
from jax.experimental.pallas import tpu as pltpu
from jax.sharding import PartitionSpec as P

ITERS = 6
NT = (((1,), (1,)), ((), ()))
TILE = 256
LIMIT = 14 * 2**20
VMEM = pl.BlockSpec(memory_space=pltpu.VMEM)
SMEM = pl.BlockSpec(memory_space=pltpu.SMEM)
HBM = pl.BlockSpec(memory_space=pltpu.HBM)


def split(x):
    hi = x.astype(jnp.bfloat16)
    lo = (x - hi.astype(jnp.float32)).astype(jnp.bfloat16)
    return hi, lo


def turn(x, heads):
    return jnp.concatenate([-x[heads:], x[:heads]], axis=0)


def split_all(src, wide, buffers, sems):
    count, rows, cols = src.shape
    depth, chunk, _ = buffers.shape
    steps = [(j, r) for j in range(count) for r in range(0, rows, chunk)]

    def copy(i):
        j, r = steps[i]
        return pltpu.make_async_copy(
            src.at[j, pl.ds(r, chunk)], buffers.at[i % depth], sems.at[i % depth]
        )

    for i in range(min(depth, len(steps))):
        copy(i).start()
    for i, (j, r) in enumerate(steps):
        copy(i).wait()
        hi, lo = split(buffers[i % depth])
        slot, c = j // 2, j % 2
        at = 2 * c * rows + r
        wide[at:at + chunk, slot * cols:(slot + 1) * cols] = hi
        wide[at + rows:at + rows + chunk, slot * cols:(slot + 1) * cols] = lo
        if i + depth < len(steps):
            copy(i + depth).start()


def put_field(lhs, slot, x):
    rows, panels = x.shape
    hi, lo = split(x)
    lhs[:rows, slot * panels:(slot + 1) * panels] = hi
    lhs[rows:, slot * panels:(slot + 1) * panels] = lo


def product(lhs, wide, heads, store):
    panels = wide.shape[0] // 4
    rows = 2 * heads

    def real(row):
        total = None
        for part in range(2):
            at = row + part * panels
            term = lax.dot_general(
                lhs[...], wide[at:at + TILE, :], NT, preferred_element_type=jnp.float32
            )
            total = term if total is None else total + term
        return total[:rows] + total[rows:]

    for start in range(0, panels, TILE):
        store(slice(start, start + TILE), real(start) + turn(real(2 * panels + start), heads))


def first_kernel(heads, inverse, field_ref, wide, out_ref, lhs, buffers, sems):
    split_all(inverse, wide, buffers, sems)
    put_field(lhs, 0, field_ref[...])

    def store(part, value):
        out_ref[:, part] = value

    product(lhs, wide, heads, store)


def split_kernel(src, field_ref, wide, same_ref, buffers, sems):
    split_all(src, wide, buffers, sems)
    same_ref[...] = field_ref[...]


def sweep_kernel(heads, slots, count, last, row_ref, *refs):
    blocks = refs[:count]
    field_ref, cross, inverse = refs[count:count + 3]
    refs = refs[count + 3:]
    if last:
        weight_ref, out_ref, part_ref, near, load, lhs, short = refs
    else:
        out_ref, near, load, lhs, short = refs
    me = lax.axis_index("body")
    lines = count // 4
    for k in range(slots):
        index = row_ref[0, k]
        dz = lax.rem(me // 4 + lines - index // 4, lines)
        at = dz * 4 + jnp.bitwise_xor(lax.rem(index, 4), lax.rem(me, 4))
        at = jnp.where(index < 0, -1, at)
        for j in range(count):
            @pl.when(at == j)
            def _():
                near[...] = blocks[j][...]

        @pl.when(index < 0)
        def _():
            near[...] = jnp.zeros_like(near)

        put_field(lhs, k, near[...])

    def store_load(part, value):
        load[:, part] = field_ref[:, part] - value

    product(lhs, cross, heads, store_load)
    put_field(short, 0, load[...])

    def store(part, value):
        out_ref[:, part] = value

    product(short, inverse, heads, store)
    if last:
        part = jnp.sum(out_ref[...] * weight_ref[...], axis=1, keepdims=True)
        part_ref[...] = jnp.broadcast_to(part, part_ref.shape)


def body(count, incident, self_inverse, cross_blocks, neighbours, panel_weight):
    _, _, heads, panels = incident.shape
    slots = cross_blocks.shape[1]
    rows = 2 * heads
    field = incident.reshape(rows, panels)
    lines = count // 4
    out = jax.ShapeDtypeStruct((rows, panels), jnp.float32)
    tiny = jax.ShapeDtypeStruct((rows, 128), jnp.float32)
    params = pltpu.CompilerParams(vmem_limit_bytes=LIMIT)
    chunk = panels // 2
    inverse, sources = pl.pallas_call(
        functools.partial(first_kernel, heads),
        in_specs=[HBM, VMEM],
        out_specs=[VMEM, VMEM],
        out_shape=[jax.ShapeDtypeStruct((4 * panels, panels), jnp.bfloat16), out],
        scratch_shapes=[
            pltpu.VMEM((2 * rows, panels), jnp.bfloat16),
            pltpu.VMEM((4, chunk, panels), jnp.float32),
            pltpu.SemaphoreType.DMA((4,)),
        ],
        compiler_params=params,
    )(pltpu.with_memory_space_constraint(self_inverse[0], pltpu.HBM), field)
    size = cross_blocks.size * 4
    all_blocks = cross_blocks[0].reshape(2 * slots, panels, panels)
    cross, same = pl.pallas_call(
        split_kernel,
        in_specs=[HBM, VMEM],
        out_specs=[VMEM, VMEM],
        out_shape=[jax.ShapeDtypeStruct((4 * panels, slots * panels), jnp.bfloat16), out],
        scratch_shapes=[
            pltpu.VMEM((6, chunk, panels), jnp.float32),
            pltpu.SemaphoreType.DMA((6,)),
        ],
        compiler_params=params,
        cost_estimate=pl.CostEstimate(flops=4 * size, bytes_accessed=size, transcendentals=0),
    )(pltpu.with_memory_space_constraint(all_blocks, pltpu.HBM), sources)

    def sweep(last, *args):
        return pl.pallas_call(
            functools.partial(sweep_kernel, heads, slots, count, last),
            in_specs=[SMEM] + [VMEM] * (len(args) - 1),
            out_specs=[VMEM, VMEM] if last else VMEM,
            out_shape=[out, tiny] if last else out,
            scratch_shapes=[
                pltpu.VMEM((rows, panels), jnp.float32),
                pltpu.VMEM((rows, panels), jnp.float32),
                pltpu.VMEM((2 * rows, slots * panels), jnp.bfloat16),
                pltpu.VMEM((2 * rows, panels), jnp.bfloat16),
            ],
            compiler_params=params,
        )(*args)

    def move(x, pairs):
        return lax.ppermute(x, "body", pairs)

    z_pairs = [[(i, (i + 4 * d) % count) for i in range(count)] for d in range(lines)]
    y_pairs = [(i, i ^ 2) for i in range(count)]
    c_pairs = [(i, i ^ 1) for i in range(count)]
    for step in range(ITERS):
        blocks = [None] * count
        own = sources if step else same
        blocks[0] = sources
        up, down = sources, sources
        for d in range(1, lines // 2 + 1):
            up = blocks[4 * d] = move(up, z_pairs[1])
            if d < lines - d:
                down = blocks[4 * (lines - d)] = move(down, z_pairs[lines - 1])
        for d in range(lines):
            blocks[4 * d + 2] = move(blocks[4 * d] if d else own, y_pairs)
        for d in range(lines):
            blocks[4 * d + 1] = move(blocks[4 * d] if d else own, c_pairs)
        for d in range(lines):
            blocks[4 * d + 3] = move(blocks[4 * d + 2], c_pairs)
        args = (neighbours, *blocks, field, cross, inverse)
        if step == ITERS - 1:
            sources, part = sweep(True, *args, panel_weight)
        else:
            sources = sweep(False, *args)
    terms = [part] + [move(part, z_pairs[d]) for d in range(1, lines)]
    while len(terms) > 1:
        half = len(terms) // 2
        terms = [terms[i] + terms[i + half] for i in range(half)]
    part = terms[0]
    part = part + move(part, y_pairs)
    part = part + move(part, c_pairs)
    farm_force = part[:, 0].reshape(1, 2, heads)
    return (sources.reshape(1, 2, heads, panels), farm_force)


def solution(mesh):
    return jax.shard_map(
        functools.partial(body, mesh.shape["body"]),
        mesh=mesh,
        in_specs=(
            P(("farm", "body"), None, None, None),
            P(("farm", "body"), None, None, None),
            P(("farm", "body"), None, None, None, None),
            P(("farm", "body"), None),
            P(("farm", "body"), None),
        ),
        out_specs=(P(("farm", "body"), None, None, None), P("farm", None, None)),
        check_vma=False,
    )
```

```python
import functools

import jax
import jax.numpy as jnp
from jax import lax
from jax.experimental import pallas as pl
from jax.experimental.pallas import tpu as pltpu
from jax.sharding import PartitionSpec as P

ITERS = 6
NT = (((1,), (1,)), ((), ()))
LIMIT = 14 * 2**20
VMEM = pl.BlockSpec(memory_space=pltpu.VMEM)
SMEM = pl.BlockSpec(memory_space=pltpu.SMEM)
HBM = pl.BlockSpec(memory_space=pltpu.HBM)


def split(x):
    hi = x.astype(jnp.bfloat16)
    lo = (x - hi.astype(jnp.float32)).astype(jnp.bfloat16)
    return hi, lo


def turn(x, heads):
    return jnp.concatenate([-x[heads:], x[:heads]], axis=0)


def split_all(src, wide, buffers, sems):
    count, rows, cols = src.shape
    depth, chunk, _ = buffers.shape
    steps = [(j, r) for j in range(count) for r in range(0, rows, chunk)]

    def copy(i):
        j, r = steps[i]
        return pltpu.make_async_copy(
            src.at[j, pl.ds(r, chunk)], buffers.at[i % depth], sems.at[i % depth]
        )

    for i in range(min(depth, len(steps))):
        copy(i).start()
    for i, (j, r) in enumerate(steps):
        copy(i).wait()
        hi, lo = split(buffers[i % depth])
        slot, c = j // 2, j % 2
        at = 2 * c * rows + r
        wide[at:at + chunk, slot * cols:(slot + 1) * cols] = hi
        wide[at + rows:at + rows + chunk, slot * cols:(slot + 1) * cols] = lo
        if i + depth < len(steps):
            copy(i + depth).start()


def put_field(lhs, slot, x):
    rows, panels = x.shape
    hi, lo = split(x)
    lhs[:rows, slot * panels:(slot + 1) * panels] = hi
    lhs[rows:, slot * panels:(slot + 1) * panels] = lo


def product(lhs, wide, heads):
    panels = wide.shape[0] // 4
    rows = 2 * heads

    def real(c):
        at = 2 * c * panels
        both = lax.dot_general(
            lhs[...], wide[at:at + 2 * panels, :], NT, preferred_element_type=jnp.float32
        )
        high = both[:rows] + both[rows:]
        return high[:, :panels] + high[:, panels:]

    return real(0) + turn(real(1), heads)


def first_kernel(heads, inverse, field_ref, wide, out_ref, lhs, buffers, sems):
    split_all(inverse, wide, buffers, sems)
    put_field(lhs, 0, field_ref[...])
    out_ref[...] = product(lhs, wide, heads)


def split_kernel(src, field_ref, wide, same_ref, buffers, sems):
    split_all(src, wide, buffers, sems)
    same_ref[...] = field_ref[...]


def after_kernel(*refs):
    del refs


def after(x, *others):
    here = pl.BlockSpec(memory_space=pl.ANY)
    return pl.pallas_call(
        after_kernel,
        in_specs=[here] * (1 + len(others)),
        out_specs=here,
        out_shape=jax.ShapeDtypeStruct(x.shape, x.dtype),
        input_output_aliases={0: 0},
        compiler_params=pltpu.CompilerParams(vmem_limit_bytes=2**20),
    )(x, *others)


def sweep_kernel(heads, slots, places, last, row_ref, *refs):
    count = len(places)
    blocks = dict(zip(places, refs[:count]))
    field_ref, cross, inverse = refs[count:count + 3]
    refs = refs[count + 3:]
    if last:
        weight_ref, out_ref, part_ref, near, lhs, short = refs
    else:
        out_ref, near, lhs, short = refs
    me = lax.axis_index("body")
    lines = count // 4
    for k in range(slots):
        index = row_ref[0, k]
        dz = lax.rem(me // 4 + lines - index // 4, lines)
        at = dz * 4 + jnp.bitwise_xor(lax.rem(index, 4), lax.rem(me, 4))
        at = jnp.where(index < 0, -1, at)
        for j in range(count):
            @pl.when(at == j)
            def _():
                near[...] = blocks[j][...]

        @pl.when(index < 0)
        def _():
            near[...] = jnp.zeros_like(near)

        put_field(lhs, k, near[...])

    put_field(short, 0, field_ref[...] - product(lhs, cross, heads))
    value = product(short, inverse, heads)
    out_ref[...] = value
    if last:
        part = jnp.sum(value * weight_ref[...], axis=1, keepdims=True)
        part_ref[...] = jnp.broadcast_to(part, part_ref.shape)


def body(count, incident, self_inverse, cross_blocks, neighbours, panel_weight):
    _, _, heads, panels = incident.shape
    slots = cross_blocks.shape[1]
    rows = 2 * heads
    field = incident.reshape(rows, panels)
    lines = count // 4
    out = jax.ShapeDtypeStruct((rows, panels), jnp.float32)
    tiny = jax.ShapeDtypeStruct((rows, 128), jnp.float32)
    params = pltpu.CompilerParams(vmem_limit_bytes=LIMIT)
    chunk = panels // 2
    inverse, sources = pl.pallas_call(
        functools.partial(first_kernel, heads),
        in_specs=[HBM, VMEM],
        out_specs=[VMEM, VMEM],
        out_shape=[jax.ShapeDtypeStruct((4 * panels, panels), jnp.bfloat16), out],
        scratch_shapes=[
            pltpu.VMEM((2 * rows, panels), jnp.bfloat16),
            pltpu.VMEM((4, chunk, panels), jnp.float32),
            pltpu.SemaphoreType.DMA((4,)),
        ],
        compiler_params=params,
    )(pltpu.with_memory_space_constraint(self_inverse[0], pltpu.HBM), field)
    size = cross_blocks.size * 4
    all_blocks = cross_blocks[0].reshape(2 * slots, panels, panels)
    cross, same = pl.pallas_call(
        split_kernel,
        in_specs=[HBM, VMEM],
        out_specs=[VMEM, VMEM],
        out_shape=[jax.ShapeDtypeStruct((4 * panels, slots * panels), jnp.bfloat16), out],
        scratch_shapes=[
            pltpu.VMEM((6, chunk, panels), jnp.float32),
            pltpu.SemaphoreType.DMA((6,)),
        ],
        compiler_params=params,
        cost_estimate=pl.CostEstimate(flops=4 * size, bytes_accessed=size, transcendentals=0),
    )(pltpu.with_memory_space_constraint(all_blocks, pltpu.HBM), sources)

    def sweep(last, *args):
        return pl.pallas_call(
            functools.partial(sweep_kernel, heads, slots, places, last),
            in_specs=[SMEM] + [VMEM] * (len(args) - 1),
            out_specs=[VMEM, VMEM] if last else VMEM,
            out_shape=[out, tiny] if last else out,
            scratch_shapes=[
                pltpu.VMEM((rows, panels), jnp.float32),
                pltpu.VMEM((2 * rows, slots * panels), jnp.bfloat16),
                pltpu.VMEM((2 * rows, panels), jnp.bfloat16),
            ],
            compiler_params=params,
        )(*args)

    def move(x, pairs):
        return lax.ppermute(x, "body", pairs)

    z_pairs = [[(i, (i + 4 * d) % count) for i in range(count)] for d in range(lines)]
    y_pairs = [(i, i ^ 2) for i in range(count)]
    c_pairs = [(i, i ^ 1) for i in range(count)]
    order = sorted(range(1, lines), key=lambda d: min(d, lines - d))
    places = [4 * d + j for d in [0] + order[::-1] for j in range(4)]
    for step in range(ITERS):
        blocks = [None] * count
        own = sources if step else same
        blocks[0] = sources
        for d in order:
            blocks[4 * d] = move(sources, z_pairs[d])
        blocks[2] = move(own, y_pairs)
        for d in order[:-1]:
            blocks[4 * d + 2] = move(blocks[4 * d], y_pairs)
        far = order[-1]
        passed = [blocks[4 * d + 2] for d in order[:-1]]
        blocks[4 * far] = after(blocks[4 * far], *passed)
        blocks[4 * far + 2] = move(blocks[4 * far], y_pairs)
        for d in [0] + order:
            blocks[4 * d + 1] = move(blocks[4 * d] if d else own, c_pairs)
            blocks[4 * d + 3] = move(blocks[4 * d + 2], c_pairs)
        args = (neighbours, *[blocks[j] for j in places], field, cross, inverse)
        if step == ITERS - 1:
            sources, part = sweep(True, *args, panel_weight)
        else:
            sources = sweep(False, *args)
    terms = [part] + [move(part, z_pairs[d]) for d in range(1, lines)]
    while len(terms) > 1:
        half = len(terms) // 2
        terms = [terms[i] + terms[i + half] for i in range(half)]
    part = terms[0]
    part = part + move(part, y_pairs)
    part = part + move(part, c_pairs)
    farm_force = part[:, 0].reshape(1, 2, heads)
    return (sources.reshape(1, 2, heads, panels), farm_force)


def solution(mesh):
    return jax.shard_map(
        functools.partial(body, mesh.shape["body"]),
        mesh=mesh,
        in_specs=(
            P(("farm", "body"), None, None, None),
            P(("farm", "body"), None, None, None),
            P(("farm", "body"), None, None, None, None),
            P(("farm", "body"), None),
            P(("farm", "body"), None),
        ),
        out_specs=(P(("farm", "body"), None, None, None), P("farm", None, None)),
        check_vma=False,
    )
```

```python
import functools

import jax
import jax.numpy as jnp
from jax import lax
from jax.experimental import pallas as pl
from jax.experimental.pallas import tpu as pltpu
from jax.sharding import PartitionSpec as P

ITERS = 6
NT = (((1,), (1,)), ((), ()))
LIMIT = 14 * 2**20
VMEM = pl.BlockSpec(memory_space=pltpu.VMEM)
SMEM = pl.BlockSpec(memory_space=pltpu.SMEM)
HBM = pl.BlockSpec(memory_space=pltpu.HBM)


def split(x):
    hi = x.astype(jnp.bfloat16)
    lo = (x - hi.astype(jnp.float32)).astype(jnp.bfloat16)
    return hi, lo


def turn(x, heads):
    return jnp.concatenate([-x[heads:], x[:heads]], axis=0)


def split_all(src, wide, buffers, sems):
    count, rows, cols = src.shape
    depth, chunk, _ = buffers.shape
    steps = [(j, r) for j in range(count) for r in range(0, rows, chunk)]

    def copy(i):
        j, r = steps[i]
        return pltpu.make_async_copy(
            src.at[j, pl.ds(r, chunk)], buffers.at[i % depth], sems.at[i % depth]
        )

    for i in range(min(depth, len(steps))):
        copy(i).start()
    for i, (j, r) in enumerate(steps):
        copy(i).wait()
        hi, lo = split(buffers[i % depth])
        slot, c = j // 2, j % 2
        at = 2 * c * rows + r
        wide[at:at + chunk, slot * cols:(slot + 1) * cols] = hi
        wide[at + rows:at + rows + chunk, slot * cols:(slot + 1) * cols] = lo
        if i + depth < len(steps):
            copy(i + depth).start()


def put_field(lhs, slot, x):
    rows, panels = x.shape
    hi, lo = split(x)
    lhs[:rows, slot * panels:(slot + 1) * panels] = hi
    lhs[rows:, slot * panels:(slot + 1) * panels] = lo


def product(lhs, wide, heads):
    panels = wide.shape[0] // 4
    rows = 2 * heads

    def real(c):
        total = None
        for part in range(2):
            at = (2 * c + part) * panels
            term = lax.dot_general(
                wide[at:at + panels, :], lhs[...], NT, preferred_element_type=jnp.float32
            )
            total = term if total is None else total + term
        flat = total.T
        return flat[:rows] + flat[rows:]

    return real(0) + turn(real(1), heads)


def first_kernel(heads, inverse, field_ref, wide, out_ref, lhs, buffers, sems):
    split_all(inverse, wide, buffers, sems)
    put_field(lhs, 0, field_ref[...])
    out_ref[...] = product(lhs, wide, heads)


def split_kernel(src, field_ref, wide, same_ref, buffers, sems):
    split_all(src, wide, buffers, sems)
    same_ref[...] = field_ref[...]


def after_kernel(*refs):
    del refs


def after(a, b, *others):
    here = pl.BlockSpec(memory_space=pl.ANY)
    like = jax.ShapeDtypeStruct(a.shape, a.dtype)
    return pl.pallas_call(
        after_kernel,
        in_specs=[here] * (2 + len(others)),
        out_specs=[here] * 2,
        out_shape=[like] * 2,
        input_output_aliases={0: 0, 1: 1},
        compiler_params=pltpu.CompilerParams(vmem_limit_bytes=2**20),
    )(a, b, *others)


def sweep_kernel(heads, slots, places, last, row_ref, *refs):
    count = len(places)
    blocks = dict(zip(places, refs[:count]))
    field_ref, cross, inverse = refs[count:count + 3]
    refs = refs[count + 3:]
    if last:
        weight_ref, out_ref, part_ref, near, lhs, short = refs
    else:
        out_ref, near, lhs, short = refs
    me = lax.axis_index("body")
    lines = count // 4
    for k in range(slots):
        index = row_ref[0, k]
        dz = lax.rem(me // 4 + lines - index // 4, lines)
        at = dz * 4 + jnp.bitwise_xor(lax.rem(index, 4), lax.rem(me, 4))
        at = jnp.where(index < 0, -1, at)
        for j in range(count):
            @pl.when(at == j)
            def _():
                near[...] = blocks[j][...]

        @pl.when(index < 0)
        def _():
            near[...] = jnp.zeros_like(near)

        put_field(lhs, k, near[...])

    put_field(short, 0, field_ref[...] - product(lhs, cross, heads))
    value = product(short, inverse, heads)
    out_ref[...] = value
    if last:
        part = jnp.sum(value * weight_ref[...], axis=1, keepdims=True)
        part_ref[...] = jnp.broadcast_to(part, part_ref.shape)


def body(count, incident, self_inverse, cross_blocks, neighbours, panel_weight):
    _, _, heads, panels = incident.shape
    slots = cross_blocks.shape[1]
    rows = 2 * heads
    field = incident.reshape(rows, panels)
    lines = count // 4
    out = jax.ShapeDtypeStruct((rows, panels), jnp.float32)
    tiny = jax.ShapeDtypeStruct((rows, 128), jnp.float32)
    params = pltpu.CompilerParams(vmem_limit_bytes=LIMIT)
    chunk = panels // 2
    inverse, sources = pl.pallas_call(
        functools.partial(first_kernel, heads),
        in_specs=[HBM, VMEM],
        out_specs=[VMEM, VMEM],
        out_shape=[jax.ShapeDtypeStruct((4 * panels, panels), jnp.bfloat16), out],
        scratch_shapes=[
            pltpu.VMEM((2 * rows, panels), jnp.bfloat16),
            pltpu.VMEM((4, chunk, panels), jnp.float32),
            pltpu.SemaphoreType.DMA((4,)),
        ],
        compiler_params=params,
    )(pltpu.with_memory_space_constraint(self_inverse[0], pltpu.HBM), field)
    size = cross_blocks.size * 4
    all_blocks = cross_blocks[0].reshape(2 * slots, panels, panels)
    cross, same = pl.pallas_call(
        split_kernel,
        in_specs=[HBM, VMEM],
        out_specs=[VMEM, VMEM],
        out_shape=[jax.ShapeDtypeStruct((4 * panels, slots * panels), jnp.bfloat16), out],
        scratch_shapes=[
            pltpu.VMEM((6, chunk, panels), jnp.float32),
            pltpu.SemaphoreType.DMA((6,)),
        ],
        compiler_params=params,
        cost_estimate=pl.CostEstimate(flops=4 * size, bytes_accessed=size, transcendentals=0),
    )(pltpu.with_memory_space_constraint(all_blocks, pltpu.HBM), sources)

    def sweep(last, *args):
        return pl.pallas_call(
            functools.partial(sweep_kernel, heads, slots, places, last),
            in_specs=[SMEM] + [VMEM] * (len(args) - 1),
            out_specs=[VMEM, VMEM] if last else VMEM,
            out_shape=[out, tiny] if last else out,
            scratch_shapes=[
                pltpu.VMEM((rows, panels), jnp.float32),
                pltpu.VMEM((2 * rows, slots * panels), jnp.bfloat16),
                pltpu.VMEM((2 * rows, panels), jnp.bfloat16),
            ],
            compiler_params=params,
        )(*args)

    def move(x, pairs):
        return lax.ppermute(x, "body", pairs)

    z_pairs = [[(i, (i + 4 * d) % count) for i in range(count)] for d in range(lines)]
    y_pairs = [(i, i ^ 2) for i in range(count)]
    c_pairs = [(i, i ^ 1) for i in range(count)]
    order = sorted(range(1, lines), key=lambda d: min(d, lines - d))
    places = [4 * d + j for d in order[::-1] + [0] for j in range(4)]
    for step in range(ITERS):
        blocks = [None] * count
        own = sources if step else same
        blocks[0] = sources
        for d in order:
            blocks[4 * d] = move(sources, z_pairs[d])
        far = order[-1]
        blocks[2] = move(own, y_pairs)
        blocks[4 * far + 2] = move(sources, [(i, j ^ 2) for i, j in z_pairs[far]])
        for d in order[:-1]:
            blocks[4 * d + 2] = move(blocks[4 * d], y_pairs)
        passed = [blocks[4 * d + 2] for d in order[:-1]]
        pair = after(blocks[4 * far], blocks[4 * far + 2], *passed)
        blocks[4 * far], blocks[4 * far + 2] = pair
        for d in [0] + order:
            blocks[4 * d + 1] = move(blocks[4 * d] if d else own, c_pairs)
            blocks[4 * d + 3] = move(blocks[4 * d + 2], c_pairs)
        args = (neighbours, *[blocks[j] for j in places], field, cross, inverse)
        if step == ITERS - 1:
            sources, part = sweep(True, *args, panel_weight)
        else:
            sources = sweep(False, *args)
    terms = [part] + [move(part, z_pairs[d]) for d in range(1, lines)]
    while len(terms) > 1:
        half = len(terms) // 2
        terms = [terms[i] + terms[i + half] for i in range(half)]
    part = terms[0]
    part = part + move(part, y_pairs)
    part = part + move(part, c_pairs)
    farm_force = part[:, 0].reshape(1, 2, heads)
    return (sources.reshape(1, 2, heads, panels), farm_force)


def solution(mesh):
    return jax.shard_map(
        functools.partial(body, mesh.shape["body"]),
        mesh=mesh,
        in_specs=(
            P(("farm", "body"), None, None, None),
            P(("farm", "body"), None, None, None),
            P(("farm", "body"), None, None, None, None),
            P(("farm", "body"), None),
            P(("farm", "body"), None),
        ),
        out_specs=(P(("farm", "body"), None, None, None), P("farm", None, None)),
        check_vma=False,
    )
```

```python
import functools

import jax
import jax.numpy as jnp
from jax import lax
from jax.experimental import pallas as pl
from jax.experimental.pallas import tpu as pltpu
from jax.sharding import PartitionSpec as P

ITERS = 6
NT = (((1,), (1,)), ((), ()))
LIMIT = 14 * 2**20
VMEM = pl.BlockSpec(memory_space=pltpu.VMEM)
SMEM = pl.BlockSpec(memory_space=pltpu.SMEM)
HBM = pl.BlockSpec(memory_space=pltpu.HBM)


def split(x):
    hi = x.astype(jnp.bfloat16)
    lo = (x - hi.astype(jnp.float32)).astype(jnp.bfloat16)
    return hi, lo


def turn(x, heads):
    return jnp.concatenate([-x[heads:], x[:heads]], axis=0)


def split_all(src, wide, buffers, sems):
    count, rows, cols = src.shape
    depth, chunk, _ = buffers.shape
    steps = [(j, r) for j in range(count) for r in range(0, rows, chunk)]

    def copy(i):
        j, r = steps[i]
        return pltpu.make_async_copy(
            src.at[j, pl.ds(r, chunk)], buffers.at[i % depth], sems.at[i % depth]
        )

    for i in range(min(depth, len(steps))):
        copy(i).start()
    for i, (j, r) in enumerate(steps):
        copy(i).wait()
        hi, lo = split(buffers[i % depth])
        slot, c = j // 2, j % 2
        at = 2 * c * rows + r
        wide[at:at + chunk, slot * cols:(slot + 1) * cols] = hi
        wide[at + rows:at + rows + chunk, slot * cols:(slot + 1) * cols] = lo
        if i + depth < len(steps):
            copy(i + depth).start()


def put_field(lhs, slot, x):
    rows, panels = x.shape
    hi, lo = split(x)
    lhs[:rows, slot * panels:(slot + 1) * panels] = hi
    lhs[rows:, slot * panels:(slot + 1) * panels] = lo


def product(lhs, wide, heads):
    panels = wide.shape[0] // 4
    rows = 2 * heads

    def real(c):
        total = None
        for part in range(2):
            at = (2 * c + part) * panels
            term = lax.dot_general(
                wide[at:at + panels, :], lhs[...], NT, preferred_element_type=jnp.float32
            )
            total = term if total is None else total + term
        flat = total.T
        return flat[:rows] + flat[rows:]

    return real(0) + turn(real(1), heads)


def first_kernel(heads, inverse, field_ref, wide, out_ref, lhs, buffers, sems):
    split_all(inverse, wide, buffers, sems)
    put_field(lhs, 0, field_ref[...])
    out_ref[...] = product(lhs, wide, heads)


def split_kernel(src, field_ref, wide, same_ref, buffers, sems):
    split_all(src, wide, buffers, sems)
    same_ref[...] = field_ref[...]


def after_kernel(*refs):
    del refs


def after(a, b, *others):
    here = pl.BlockSpec(memory_space=pl.ANY)
    like = jax.ShapeDtypeStruct(a.shape, a.dtype)
    return pl.pallas_call(
        after_kernel,
        in_specs=[here] * (2 + len(others)),
        out_specs=[here] * 2,
        out_shape=[like] * 2,
        input_output_aliases={0: 0, 1: 1},
        compiler_params=pltpu.CompilerParams(vmem_limit_bytes=2**20),
    )(a, b, *others)


def sweep_kernel(heads, slots, lines, places, last, row_ref, *refs):
    held = refs[:len(places)]
    count = 4 * lines
    field_ref, cross, inverse = refs[len(places):len(places) + 3]
    refs = refs[len(places) + 3:]
    if last:
        weight_ref, out_ref, part_ref, near, lhs, short = refs
    else:
        out_ref, near, lhs, short = refs
    me = lax.axis_index("body")
    for k in range(slots):
        index = row_ref[0, k]
        dz = lax.rem(me // 4 + lines - index // 4, lines)
        at = dz * 4 + jnp.bitwise_xor(lax.rem(index, 4), lax.rem(me, 4))
        at = jnp.where(index < 0, -1, at)
        for (place, parity), block in zip(places, held):
            match = at == place
            if parity is not None:
                match = match & (lax.rem(me, 2) == parity)

            @pl.when(match)
            def _():
                near[...] = block[...]

        @pl.when(index < 0)
        def _():
            near[...] = jnp.zeros_like(near)

        put_field(lhs, k, near[...])

    put_field(short, 0, field_ref[...] - product(lhs, cross, heads))
    value = product(short, inverse, heads)
    out_ref[...] = value
    if last:
        part = jnp.sum(value * weight_ref[...], axis=1, keepdims=True)
        part_ref[...] = jnp.broadcast_to(part, part_ref.shape)


def body(count, incident, self_inverse, cross_blocks, neighbours, panel_weight):
    _, _, heads, panels = incident.shape
    slots = cross_blocks.shape[1]
    rows = 2 * heads
    field = incident.reshape(rows, panels)
    lines = count // 4
    out = jax.ShapeDtypeStruct((rows, panels), jnp.float32)
    tiny = jax.ShapeDtypeStruct((rows, 128), jnp.float32)
    params = pltpu.CompilerParams(vmem_limit_bytes=LIMIT)
    chunk = panels // 2
    inverse, sources = pl.pallas_call(
        functools.partial(first_kernel, heads),
        in_specs=[HBM, VMEM],
        out_specs=[VMEM, VMEM],
        out_shape=[jax.ShapeDtypeStruct((4 * panels, panels), jnp.bfloat16), out],
        scratch_shapes=[
            pltpu.VMEM((2 * rows, panels), jnp.bfloat16),
            pltpu.VMEM((4, chunk, panels), jnp.float32),
            pltpu.SemaphoreType.DMA((4,)),
        ],
        compiler_params=params,
    )(pltpu.with_memory_space_constraint(self_inverse[0], pltpu.HBM), field)
    size = cross_blocks.size * 4
    all_blocks = cross_blocks[0].reshape(2 * slots, panels, panels)
    cross, same = pl.pallas_call(
        split_kernel,
        in_specs=[HBM, VMEM],
        out_specs=[VMEM, VMEM],
        out_shape=[jax.ShapeDtypeStruct((4 * panels, slots * panels), jnp.bfloat16), out],
        scratch_shapes=[
            pltpu.VMEM((6, chunk, panels), jnp.float32),
            pltpu.SemaphoreType.DMA((6,)),
        ],
        compiler_params=params,
        cost_estimate=pl.CostEstimate(flops=4 * size, bytes_accessed=size, transcendentals=0),
    )(pltpu.with_memory_space_constraint(all_blocks, pltpu.HBM), sources)

    def sweep(last, *args):
        return pl.pallas_call(
            functools.partial(sweep_kernel, heads, slots, lines, places, last),
            in_specs=[SMEM] + [VMEM] * (len(args) - 1),
            out_specs=[VMEM, VMEM] if last else VMEM,
            out_shape=[out, tiny] if last else out,
            scratch_shapes=[
                pltpu.VMEM((rows, panels), jnp.float32),
                pltpu.VMEM((2 * rows, slots * panels), jnp.bfloat16),
                pltpu.VMEM((2 * rows, panels), jnp.bfloat16),
            ],
            compiler_params=params,
        )(*args)

    def move(x, pairs):
        return lax.ppermute(x, "body", pairs)

    z_pairs = [[(i, (i + 4 * d) % count) for i in range(count)] for d in range(lines)]
    y_pairs = [(i, i ^ 2) for i in range(count)]
    c_pairs = [(i, i ^ 1) for i in range(count)]
    order = sorted(range(1, lines), key=lambda d: min(d, lines - d))
    near_first, far = order[:-1], order[-1]
    rest = [4 * d + j for d in near_first[::-1] + [0] for j in range(4)]
    places = [(4 * far, None), (4 * far + 1, None)]
    places += [(4 * far + 2, 1), (4 * far + 2, 0), (4 * far + 3, 0), (4 * far + 3, 1)]
    places += [(j, None) for j in rest]
    direct = [(i, j ^ 2) for i, j in z_pairs[far] if i % 2]
    for step in range(ITERS):
        own = sources if step else same
        blocks = {0: sources}
        for d in near_first:
            blocks[4 * d] = move(sources, z_pairs[d])
        blocks[2] = move(own, y_pairs)
        straight = move(own, direct)
        middle = move(own, z_pairs[far])
        for d in near_first:
            blocks[4 * d + 2] = move(blocks[4 * d], y_pairs)
        passed = [blocks[4 * d + 2] for d in near_first]
        middle, straight = after(middle, straight, *passed)
        turned = move(middle, [p for p in y_pairs if p[0] % 2 == 0])
        for d in [0] + near_first:
            blocks[4 * d + 1] = move(blocks[4 * d] if d else own, c_pairs)
            blocks[4 * d + 3] = move(blocks[4 * d + 2], c_pairs)
        held = [middle, move(middle, c_pairs), straight, turned]
        held.append(move(straight, [p for p in c_pairs if p[0] % 2]))
        held.append(move(turned, [p for p in c_pairs if p[0] % 2 == 0]))
        held += [blocks[j] for j in rest]
        args = (neighbours, *held, field, cross, inverse)
        if step == ITERS - 1:
            sources, part = sweep(True, *args, panel_weight)
        else:
            sources = sweep(False, *args)
    terms = [part] + [move(part, z_pairs[d]) for d in range(1, lines)]
    while len(terms) > 1:
        half = len(terms) // 2
        terms = [terms[i] + terms[i + half] for i in range(half)]
    part = terms[0]
    part = part + move(part, y_pairs)
    part = part + move(part, c_pairs)
    farm_force = part[:, 0].reshape(1, 2, heads)
    return (sources.reshape(1, 2, heads, panels), farm_force)


def solution(mesh):
    return jax.shard_map(
        functools.partial(body, mesh.shape["body"]),
        mesh=mesh,
        in_specs=(
            P(("farm", "body"), None, None, None),
            P(("farm", "body"), None, None, None),
            P(("farm", "body"), None, None, None, None),
            P(("farm", "body"), None),
            P(("farm", "body"), None),
        ),
        out_specs=(P(("farm", "body"), None, None, None), P("farm", None, None)),
        check_vma=False,
    )
```

```python
import functools

import jax
import jax.numpy as jnp
from jax import lax
from jax.experimental import pallas as pl
from jax.experimental.pallas import tpu as pltpu
from jax.sharding import PartitionSpec as P

ITERS = 6
NT = (((1,), (1,)), ((), ()))
LIMIT = 14 * 2**20
VMEM = pl.BlockSpec(memory_space=pltpu.VMEM)
SMEM = pl.BlockSpec(memory_space=pltpu.SMEM)
HBM = pl.BlockSpec(memory_space=pltpu.HBM)


def split(x):
    hi = x.astype(jnp.bfloat16)
    lo = (x - hi.astype(jnp.float32)).astype(jnp.bfloat16)
    return hi, lo


def turn(x, heads):
    return jnp.concatenate([-x[heads:], x[:heads]], axis=0)


def split_all(src, wide, buffers, sems, done=None):
    count, rows, cols = src.shape
    depth, chunk, _ = buffers.shape
    steps = [(j, r) for j in range(count) for r in range(0, rows, chunk)]

    def copy(i):
        j, r = steps[i]
        return pltpu.make_async_copy(
            src.at[j, pl.ds(r, chunk)], buffers.at[i % depth], sems.at[i % depth]
        )

    for i in range(min(depth, len(steps))):
        copy(i).start()
    for i, (j, r) in enumerate(steps):
        copy(i).wait()
        hi, lo = split(buffers[i % depth])
        slot, c = j // 2, j % 2
        at = 2 * c * rows + r
        wide[at:at + chunk, slot * cols:(slot + 1) * cols] = hi
        wide[at + rows:at + rows + chunk, slot * cols:(slot + 1) * cols] = lo
        if i + depth < len(steps):
            copy(i + depth).start()
        if done is not None and r + chunk == rows:
            done(j)


def put_field(lhs, slot, x):
    rows, panels = x.shape
    hi, lo = split(x)
    lhs[:rows, slot * panels:(slot + 1) * panels] = hi
    lhs[rows:, slot * panels:(slot + 1) * panels] = lo


def real_product(c, lhs, wide, rows):
    panels = wide.shape[0] // 4
    total = None
    for part in range(2):
        at = (2 * c + part) * panels
        term = lax.dot_general(
            wide[at:at + panels, :], lhs[...], NT, preferred_element_type=jnp.float32
        )
        total = term if total is None else total + term
    flat = total.T
    return flat[:rows] + flat[rows:]


def product(lhs, wide, heads):
    first = real_product(0, lhs, wide, 2 * heads)
    return first + turn(real_product(1, lhs, wide, 2 * heads), heads)


def first_kernel(heads, inverse, field_hbm, wide, out_ref, field, lhs, buffers, sems, sem):
    load = pltpu.make_async_copy(field_hbm, field, sem)
    load.start()

    def done(c):
        if c == 0:
            load.wait()
            put_field(lhs, 0, field[...])
            out_ref[...] = real_product(0, lhs, wide, 2 * heads)
        else:
            out_ref[...] += turn(real_product(1, lhs, wide, 2 * heads), heads)

    split_all(inverse, wide, buffers, sems, done)


def split_kernel(src, field_ref, wide, same_ref, buffers, sems):
    split_all(src, wide, buffers, sems)
    same_ref[...] = field_ref[...]


def after_kernel(*refs):
    del refs


def after(a, b, *others):
    here = pl.BlockSpec(memory_space=pl.ANY)
    like = jax.ShapeDtypeStruct(a.shape, a.dtype)
    return pl.pallas_call(
        after_kernel,
        in_specs=[here] * (2 + len(others)),
        out_specs=[here] * 2,
        out_shape=[like] * 2,
        input_output_aliases={0: 0, 1: 1},
        compiler_params=pltpu.CompilerParams(vmem_limit_bytes=2**20),
    )(a, b, *others)


def sweep_kernel(heads, slots, places, last, row_ref, *refs):
    count = len(places)
    blocks = dict(zip(places, refs[:count]))
    field_ref, cross, inverse = refs[count:count + 3]
    refs = refs[count + 3:]
    if last:
        weight_ref, out_ref, part_ref, near, lhs, short = refs
    else:
        out_ref, near, lhs, short = refs
    me = lax.axis_index("body")
    lines = count // 4
    for k in range(slots):
        index = row_ref[0, k]
        dz = lax.rem(me // 4 + lines - index // 4, lines)
        at = dz * 4 + jnp.bitwise_xor(lax.rem(index, 4), lax.rem(me, 4))
        at = jnp.where(index < 0, -1, at)
        for j in range(count):
            @pl.when(at == j)
            def _():
                near[...] = blocks[j][...]

        @pl.when(index < 0)
        def _():
            near[...] = jnp.zeros_like(near)

        put_field(lhs, k, near[...])

    put_field(short, 0, field_ref[...] - product(lhs, cross, heads))
    value = product(short, inverse, heads)
    out_ref[...] = value
    if last:
        for c in range(2):
            part_ref[c:c + 1, :] = lax.dot_general(
                weight_ref[...], value[c * heads:(c + 1) * heads], NT,
                precision=lax.Precision.HIGHEST, preferred_element_type=jnp.float32,
            )


def body(count, incident, self_inverse, cross_blocks, neighbours, panel_weight):
    _, _, heads, panels = incident.shape
    slots = cross_blocks.shape[1]
    rows = 2 * heads
    field = incident.reshape(rows, panels)
    lines = count // 4
    out = jax.ShapeDtypeStruct((rows, panels), jnp.float32)
    tiny = jax.ShapeDtypeStruct((2, heads), jnp.float32)
    params = pltpu.CompilerParams(vmem_limit_bytes=LIMIT)
    chunk = panels // 2
    inverse, sources = pl.pallas_call(
        functools.partial(first_kernel, heads),
        in_specs=[HBM, HBM],
        out_specs=[VMEM, VMEM],
        out_shape=[jax.ShapeDtypeStruct((4 * panels, panels), jnp.bfloat16), out],
        scratch_shapes=[
            pltpu.VMEM((rows, panels), jnp.float32),
            pltpu.VMEM((2 * rows, panels), jnp.bfloat16),
            pltpu.VMEM((4, chunk, panels), jnp.float32),
            pltpu.SemaphoreType.DMA((4,)),
            pltpu.SemaphoreType.DMA,
        ],
        compiler_params=params,
    )(
        pltpu.with_memory_space_constraint(self_inverse[0], pltpu.HBM),
        pltpu.with_memory_space_constraint(field, pltpu.HBM),
    )
    size = cross_blocks.size * 4
    all_blocks = cross_blocks[0].reshape(2 * slots, panels, panels)
    cross, same = pl.pallas_call(
        split_kernel,
        in_specs=[HBM, VMEM],
        out_specs=[VMEM, VMEM],
        out_shape=[jax.ShapeDtypeStruct((4 * panels, slots * panels), jnp.bfloat16), out],
        scratch_shapes=[
            pltpu.VMEM((6, chunk, panels), jnp.float32),
            pltpu.SemaphoreType.DMA((6,)),
        ],
        compiler_params=params,
        cost_estimate=pl.CostEstimate(flops=4 * size, bytes_accessed=size, transcendentals=0),
    )(pltpu.with_memory_space_constraint(all_blocks, pltpu.HBM), sources)

    def sweep(last, *args):
        return pl.pallas_call(
            functools.partial(sweep_kernel, heads, slots, places, last),
            in_specs=[SMEM] + [VMEM] * (len(args) - 1),
            out_specs=[VMEM, VMEM] if last else VMEM,
            out_shape=[out, tiny] if last else out,
            scratch_shapes=[
                pltpu.VMEM((rows, panels), jnp.float32),
                pltpu.VMEM((2 * rows, slots * panels), jnp.bfloat16),
                pltpu.VMEM((2 * rows, panels), jnp.bfloat16),
            ],
            compiler_params=params,
        )(*args)

    def move(x, pairs):
        return lax.ppermute(x, "body", pairs)

    z_pairs = [[(i, (i + 4 * d) % count) for i in range(count)] for d in range(lines)]
    y_pairs = [(i, i ^ 2) for i in range(count)]
    c_pairs = [(i, i ^ 1) for i in range(count)]
    order = sorted(range(1, lines), key=lambda d: min(d, lines - d))
    places = [4 * d + j for d in order[::-1] + [0] for j in range(4)]
    for step in range(ITERS):
        blocks = [None] * count
        own = sources if step else same
        blocks[0] = sources
        for d in order:
            blocks[4 * d] = move(own if d == order[-1] else sources, z_pairs[d])
        far = order[-1]
        blocks[2] = move(own, y_pairs)
        blocks[4 * far + 2] = move(own, [(i, j ^ 2) for i, j in z_pairs[far]])
        for d in order[:-1]:
            blocks[4 * d + 2] = move(blocks[4 * d], y_pairs)
        passed = [blocks[4 * d + 2] for d in order[:-1]]
        pair = after(blocks[4 * far], blocks[4 * far + 2], *passed)
        blocks[4 * far], blocks[4 * far + 2] = pair
        for d in [0] + order:
            blocks[4 * d + 1] = move(blocks[4 * d] if d else own, c_pairs)
            blocks[4 * d + 3] = move(blocks[4 * d + 2], c_pairs)
        args = (neighbours, *[blocks[j] for j in places], field, cross, inverse)
        if step == ITERS - 1:
            sources, part = sweep(True, *args, panel_weight)
        else:
            sources = sweep(False, *args)
    terms = [part] + [move(part, z_pairs[d]) for d in range(1, lines)]
    while len(terms) > 1:
        half = len(terms) // 2
        terms = [terms[i] + terms[i + half] for i in range(half)]
    part = terms[0]
    part = part + move(part, y_pairs)
    part = part + move(part, c_pairs)
    return (sources.reshape(1, 2, heads, panels), part[None])


def solution(mesh):
    return jax.shard_map(
        functools.partial(body, mesh.shape["body"]),
        mesh=mesh,
        in_specs=(
            P(("farm", "body"), None, None, None),
            P(("farm", "body"), None, None, None),
            P(("farm", "body"), None, None, None, None),
            P(("farm", "body"), None),
            P(("farm", "body"), None),
        ),
        out_specs=(P(("farm", "body"), None, None, None), P("farm", None, None)),
        check_vma=False,
    )
```

```python
import functools

import jax
import jax.numpy as jnp
from jax import lax
from jax.experimental import pallas as pl
from jax.experimental.pallas import tpu as pltpu
from jax.sharding import PartitionSpec as P

ITERS = 6
NT = (((1,), (1,)), ((), ()))
LIMIT = 14 * 2**20
VMEM = pl.BlockSpec(memory_space=pltpu.VMEM)
SMEM = pl.BlockSpec(memory_space=pltpu.SMEM)
HBM = pl.BlockSpec(memory_space=pltpu.HBM)


def split(x):
    hi = x.astype(jnp.bfloat16)
    lo = (x - hi.astype(jnp.float32)).astype(jnp.bfloat16)
    return hi, lo


def turn(x, heads):
    return jnp.concatenate([-x[heads:], x[:heads]], axis=0)


def split_all(src, wide, buffers, sems, base=0):
    _, rows, cols = src.shape
    count = 2 * wide.shape[1] // cols
    depth, chunk, _ = buffers.shape
    steps = [(j, r) for j in range(count) for r in range(0, rows, chunk)]

    def copy(i):
        j, r = steps[i]
        return pltpu.make_async_copy(
            src.at[base + j, pl.ds(r, chunk)], buffers.at[i % depth], sems.at[i % depth]
        )

    for i in range(min(depth, len(steps))):
        copy(i).start()
    for i, (j, r) in enumerate(steps):
        copy(i).wait()
        hi, lo = split(buffers[i % depth])
        slot, c = j // 2, j % 2
        at = 2 * c * rows + r
        wide[at:at + chunk, slot * cols:(slot + 1) * cols] = hi
        wide[at + rows:at + rows + chunk, slot * cols:(slot + 1) * cols] = lo
        if i + depth < len(steps):
            copy(i + depth).start()


def put_field(lhs, slot, x):
    rows, panels = x.shape
    hi, lo = split(x)
    lhs[:rows, slot * panels:(slot + 1) * panels] = hi
    lhs[rows:, slot * panels:(slot + 1) * panels] = lo


def product(lhs, wides, heads):
    panels = wides[0].shape[0] // 4
    rows = 2 * heads

    def real(c):
        total = None
        for part in range(2):
            row, at = (2 * c + part) * panels, 0
            for wide in wides:
                width = wide.shape[1]
                term = lax.dot_general(
                    wide[row:row + panels, :], lhs[:, at:at + width], NT,
                    preferred_element_type=jnp.float32,
                )
                total = term if total is None else total + term
                at += width
        flat = total.T
        return flat[:rows] + flat[rows:]

    return real(0) + turn(real(1), heads)


def first_kernel(heads, inverse, field_ref, wide, out_ref, lhs, buffers, sems):
    split_all(inverse, wide, buffers, sems)
    put_field(lhs, 0, field_ref[...])
    out_ref[...] = product(lhs, [wide], heads)


def near_kernel(src, field_ref, wide, same_ref, buffers, sems):
    split_all(src, wide, buffers, sems)
    same_ref[...] = field_ref[...]


def late_kernel(base, src, waited, wide, buffers, sems):
    del waited
    split_all(src, wide, buffers, sems, base)


def after_kernel(*refs):
    del refs


def after(a, b, *others):
    here = pl.BlockSpec(memory_space=pl.ANY)
    like = jax.ShapeDtypeStruct(a.shape, a.dtype)
    return pl.pallas_call(
        after_kernel,
        in_specs=[here] * (2 + len(others)),
        out_specs=[here] * 2,
        out_shape=[like] * 2,
        input_output_aliases={0: 0, 1: 1},
        compiler_params=pltpu.CompilerParams(vmem_limit_bytes=2**20),
    )(a, b, *others)


def sweep_kernel(heads, slots, places, last, row_ref, *refs):
    count = len(places)
    blocks = dict(zip(places, refs[:count]))
    field_ref, cross_a, cross_b, inverse = refs[count:count + 4]
    refs = refs[count + 4:]
    if last:
        weight_ref, out_ref, part_ref, near, lhs, short = refs
    else:
        out_ref, near, lhs, short = refs
    me = lax.axis_index("body")
    lines = count // 4
    for k in range(slots):
        index = row_ref[0, k]
        dz = lax.rem(me // 4 + lines - index // 4, lines)
        at = dz * 4 + jnp.bitwise_xor(lax.rem(index, 4), lax.rem(me, 4))
        at = jnp.where(index < 0, -1, at)
        for j in range(count):
            @pl.when(at == j)
            def _():
                near[...] = blocks[j][...]

        @pl.when(index < 0)
        def _():
            near[...] = jnp.zeros_like(near)

        put_field(lhs, k, near[...])

    put_field(short, 0, field_ref[...] - product(lhs, [cross_a, cross_b], heads))
    value = product(short, [inverse], heads)
    out_ref[...] = value
    if last:
        for c in range(2):
            part_ref[c:c + 1, :] = lax.dot_general(
                weight_ref[...], value[c * heads:(c + 1) * heads], NT,
                precision=lax.Precision.HIGHEST, preferred_element_type=jnp.float32,
            )


def body(count, incident, self_inverse, cross_blocks, neighbours, panel_weight):
    _, _, heads, panels = incident.shape
    slots = cross_blocks.shape[1]
    rows = 2 * heads
    field = incident.reshape(rows, panels)
    lines = count // 4
    out = jax.ShapeDtypeStruct((rows, panels), jnp.float32)
    tiny = jax.ShapeDtypeStruct((2, heads), jnp.float32)
    params = pltpu.CompilerParams(vmem_limit_bytes=LIMIT)
    chunk = panels // 2
    inverse, sources = pl.pallas_call(
        functools.partial(first_kernel, heads),
        in_specs=[HBM, VMEM],
        out_specs=[VMEM, VMEM],
        out_shape=[jax.ShapeDtypeStruct((4 * panels, panels), jnp.bfloat16), out],
        scratch_shapes=[
            pltpu.VMEM((2 * rows, panels), jnp.bfloat16),
            pltpu.VMEM((4, chunk, panels), jnp.float32),
            pltpu.SemaphoreType.DMA((4,)),
        ],
        compiler_params=params,
    )(pltpu.with_memory_space_constraint(self_inverse[0], pltpu.HBM), field)
    early = slots // 2
    all_blocks = pltpu.with_memory_space_constraint(
        cross_blocks[0].reshape(2 * slots, panels, panels), pltpu.HBM
    )
    scratch = [pltpu.VMEM((6, chunk, panels), jnp.float32), pltpu.SemaphoreType.DMA((6,))]

    def cost(count):
        size = count * 8 * panels * panels
        return pl.CostEstimate(flops=4 * size, bytes_accessed=size, transcendentals=0)

    cross_a, same = pl.pallas_call(
        near_kernel,
        in_specs=[HBM, VMEM],
        out_specs=[VMEM, VMEM],
        out_shape=[jax.ShapeDtypeStruct((4 * panels, early * panels), jnp.bfloat16), out],
        scratch_shapes=scratch,
        compiler_params=params,
        cost_estimate=cost(early),
    )(all_blocks, sources)
    split_late = pl.pallas_call(
        functools.partial(late_kernel, 2 * early),
        in_specs=[HBM, pl.BlockSpec(memory_space=pl.ANY)],
        out_specs=VMEM,
        out_shape=jax.ShapeDtypeStruct((4 * panels, (slots - early) * panels), jnp.bfloat16),
        scratch_shapes=scratch,
        compiler_params=params,
        cost_estimate=cost(slots - early),
    )

    def sweep(last, *args):
        return pl.pallas_call(
            functools.partial(sweep_kernel, heads, slots, places, last),
            in_specs=[SMEM] + [VMEM] * (len(args) - 1),
            out_specs=[VMEM, VMEM] if last else VMEM,
            out_shape=[out, tiny] if last else out,
            scratch_shapes=[
                pltpu.VMEM((rows, panels), jnp.float32),
                pltpu.VMEM((2 * rows, slots * panels), jnp.bfloat16),
                pltpu.VMEM((2 * rows, panels), jnp.bfloat16),
            ],
            compiler_params=params,
        )(*args)

    def move(x, pairs):
        return lax.ppermute(x, "body", pairs)

    z_pairs = [[(i, (i + 4 * d) % count) for i in range(count)] for d in range(lines)]
    y_pairs = [(i, i ^ 2) for i in range(count)]
    c_pairs = [(i, i ^ 1) for i in range(count)]
    order = sorted(range(1, lines), key=lambda d: min(d, lines - d))
    places = [4 * d + j for d in order[::-1] + [0] for j in range(4)]
    for step in range(ITERS):
        blocks = [None] * count
        own = sources if step else same
        blocks[0] = sources
        for d in order:
            blocks[4 * d] = move(own if d == order[-1] else sources, z_pairs[d])
        far = order[-1]
        blocks[2] = move(sources, y_pairs)
        if not step:
            cross_b = split_late(all_blocks, same)
            ends = [4 * order[0], 4 * order[-2]]
            blocks[ends[0]], blocks[ends[1]] = after(*[blocks[e] for e in ends], cross_b)
        blocks[4 * far + 2] = move(own, [(i, j ^ 2) for i, j in z_pairs[far]])
        for d in order[:-1]:
            blocks[4 * d + 2] = move(blocks[4 * d], y_pairs)
        passed = [blocks[4 * d + 2] for d in order[:-1]]
        pair = after(blocks[4 * far], blocks[4 * far + 2], *passed)
        blocks[4 * far], blocks[4 * far + 2] = pair
        for d in [0] + order:
            blocks[4 * d + 1] = move(blocks[4 * d], c_pairs)
            blocks[4 * d + 3] = move(blocks[4 * d + 2], c_pairs)
        args = (neighbours, *[blocks[j] for j in places], field, cross_a, cross_b, inverse)
        if step == ITERS - 1:
            sources, part = sweep(True, *args, panel_weight)
        else:
            sources = sweep(False, *args)
    terms = [part] + [move(part, z_pairs[d]) for d in range(1, lines)]
    while len(terms) > 1:
        half = len(terms) // 2
        terms = [terms[i] + terms[i + half] for i in range(half)]
    part = terms[0]
    part = part + move(part, y_pairs)
    part = part + move(part, c_pairs)
    return (sources.reshape(1, 2, heads, panels), part[None])


def solution(mesh):
    return jax.shard_map(
        functools.partial(body, mesh.shape["body"]),
        mesh=mesh,
        in_specs=(
            P(("farm", "body"), None, None, None),
            P(("farm", "body"), None, None, None),
            P(("farm", "body"), None, None, None, None),
            P(("farm", "body"), None),
            P(("farm", "body"), None),
        ),
        out_specs=(P(("farm", "body"), None, None, None), P("farm", None, None)),
        check_vma=False,
    )
```

```python
import functools

import jax
import jax.numpy as jnp
from jax import lax
from jax.experimental import pallas as pl
from jax.experimental.pallas import tpu as pltpu
from jax.sharding import PartitionSpec as P

ITERS = 6
NT = (((1,), (1,)), ((), ()))
LIMIT = 14 * 2**20
VMEM = pl.BlockSpec(memory_space=pltpu.VMEM)
SMEM = pl.BlockSpec(memory_space=pltpu.SMEM)
HBM = pl.BlockSpec(memory_space=pltpu.HBM)


def split(x):
    hi = x.astype(jnp.bfloat16)
    lo = (x - hi.astype(jnp.float32)).astype(jnp.bfloat16)
    return hi, lo


def turn(x, heads):
    return jnp.concatenate([-x[heads:], x[:heads]], axis=0)


def split_all(src, wide, buffers, sems, base=0):
    _, rows, cols = src.shape
    count = 2 * wide.shape[1] // cols
    depth, chunk, _ = buffers.shape
    steps = [(j, r) for j in range(count) for r in range(0, rows, chunk)]

    def copy(i):
        j, r = steps[i]
        return pltpu.make_async_copy(
            src.at[base + j, pl.ds(r, chunk)], buffers.at[i % depth], sems.at[i % depth]
        )

    for i in range(min(depth, len(steps))):
        copy(i).start()
    for i, (j, r) in enumerate(steps):
        copy(i).wait()
        hi, lo = split(buffers[i % depth])
        slot, c = j // 2, j % 2
        at = 2 * c * rows + r
        wide[at:at + chunk, slot * cols:(slot + 1) * cols] = hi
        wide[at + rows:at + rows + chunk, slot * cols:(slot + 1) * cols] = lo
        if i + depth < len(steps):
            copy(i + depth).start()


def put_field(lhs, slot, x):
    rows, panels = x.shape
    hi, lo = split(x)
    lhs[:rows, slot * panels:(slot + 1) * panels] = hi
    lhs[rows:, slot * panels:(slot + 1) * panels] = lo


def product(lhs, wides, heads):
    panels = wides[0].shape[0] // 4
    rows = 2 * heads

    def real(c):
        total = None
        for part in range(2):
            row, at = (2 * c + part) * panels, 0
            for wide in wides:
                width = wide.shape[1]
                term = lax.dot_general(
                    wide[row:row + panels, :], lhs[:, at:at + width], NT,
                    preferred_element_type=jnp.float32,
                )
                total = term if total is None else total + term
                at += width
        flat = total.T
        return flat[:rows] + flat[rows:]

    return real(0) + turn(real(1), heads)


def first_kernel(heads, inverse, field_ref, wide, out_ref, lhs, buffers, sems):
    split_all(inverse, wide, buffers, sems)
    put_field(lhs, 0, field_ref[...])
    out_ref[...] = product(lhs, [wide], heads)


def near_kernel(src, field_ref, wide, same_ref, buffers, sems):
    split_all(src, wide, buffers, sems)
    same_ref[...] = field_ref[...]


def late_kernel(base, src, waited, wide, buffers, sems):
    del waited
    split_all(src, wide, buffers, sems, base)


def after_kernel(*refs):
    del refs


def after(a, b, *others):
    here = pl.BlockSpec(memory_space=pl.ANY)
    like = jax.ShapeDtypeStruct(a.shape, a.dtype)
    return pl.pallas_call(
        after_kernel,
        in_specs=[here] * (2 + len(others)),
        out_specs=[here] * 2,
        out_shape=[like] * 2,
        input_output_aliases={0: 0, 1: 1},
        compiler_params=pltpu.CompilerParams(vmem_limit_bytes=2**20),
    )(a, b, *others)


def sweep_kernel(heads, slots, places, last, row_ref, *refs):
    count = len(places)
    blocks = dict(zip(places, refs[:count]))
    field_ref, cross_a, cross_b, inverse = refs[count:count + 4]
    refs = refs[count + 4:]
    if last:
        weight_ref, out_ref, part_ref, near, lhs, short = refs
    else:
        out_ref, near, lhs, short = refs
    me = lax.axis_index("body")
    lines = count // 4
    for k in range(slots):
        index = row_ref[0, k]
        dz = lax.rem(me // 4 + lines - index // 4, lines)
        at = dz * 4 + jnp.bitwise_xor(lax.rem(index, 4), lax.rem(me, 4))
        at = jnp.where(index < 0, -1, at)
        for j in range(count):
            @pl.when(at == j)
            def _():
                near[...] = blocks[j][...]

        @pl.when(index < 0)
        def _():
            near[...] = jnp.zeros_like(near)

        put_field(lhs, k, near[...])

    put_field(short, 0, field_ref[...] - product(lhs, [cross_a, cross_b], heads))
    value = product(short, [inverse], heads)
    out_ref[...] = value
    if last:
        for c in range(2):
            part_ref[c:c + 1, :] = lax.dot_general(
                weight_ref[...], value[c * heads:(c + 1) * heads], NT,
                precision=lax.Precision.HIGHEST, preferred_element_type=jnp.float32,
            )


def body(count, incident, self_inverse, cross_blocks, neighbours, panel_weight):
    _, _, heads, panels = incident.shape
    slots = cross_blocks.shape[1]
    rows = 2 * heads
    field = incident.reshape(rows, panels)
    lines = count // 4
    out = jax.ShapeDtypeStruct((rows, panels), jnp.float32)
    tiny = jax.ShapeDtypeStruct((2, heads), jnp.float32)
    params = pltpu.CompilerParams(vmem_limit_bytes=LIMIT)
    chunk = panels // 2
    inverse, sources = pl.pallas_call(
        functools.partial(first_kernel, heads),
        in_specs=[HBM, VMEM],
        out_specs=[VMEM, VMEM],
        out_shape=[jax.ShapeDtypeStruct((4 * panels, panels), jnp.bfloat16), out],
        scratch_shapes=[
            pltpu.VMEM((2 * rows, panels), jnp.bfloat16),
            pltpu.VMEM((4, chunk, panels), jnp.float32),
            pltpu.SemaphoreType.DMA((4,)),
        ],
        compiler_params=params,
    )(pltpu.with_memory_space_constraint(self_inverse[0], pltpu.HBM), field)
    early = slots // 2
    all_blocks = pltpu.with_memory_space_constraint(
        cross_blocks[0].reshape(2 * slots, panels, panels), pltpu.HBM
    )
    scratch = [pltpu.VMEM((6, chunk, panels), jnp.float32), pltpu.SemaphoreType.DMA((6,))]

    def cost(count):
        size = count * 8 * panels * panels
        return pl.CostEstimate(flops=4 * size, bytes_accessed=size, transcendentals=0)

    cross_a, same = pl.pallas_call(
        near_kernel,
        in_specs=[HBM, VMEM],
        out_specs=[VMEM, VMEM],
        out_shape=[jax.ShapeDtypeStruct((4 * panels, early * panels), jnp.bfloat16), out],
        scratch_shapes=scratch,
        compiler_params=params,
        cost_estimate=cost(early),
    )(all_blocks, sources)
    split_late = pl.pallas_call(
        functools.partial(late_kernel, 2 * early),
        in_specs=[HBM, pl.BlockSpec(memory_space=pl.ANY)],
        out_specs=VMEM,
        out_shape=jax.ShapeDtypeStruct((4 * panels, (slots - early) * panels), jnp.bfloat16),
        scratch_shapes=scratch,
        compiler_params=params,
        cost_estimate=cost(slots - early),
    )

    def sweep(last, *args):
        return pl.pallas_call(
            functools.partial(sweep_kernel, heads, slots, places, last),
            in_specs=[SMEM] + [VMEM] * (len(args) - 1),
            out_specs=[VMEM, VMEM] if last else VMEM,
            out_shape=[out, tiny] if last else out,
            scratch_shapes=[
                pltpu.VMEM((rows, panels), jnp.float32),
                pltpu.VMEM((2 * rows, slots * panels), jnp.bfloat16),
                pltpu.VMEM((2 * rows, panels), jnp.bfloat16),
            ],
            compiler_params=params,
        )(*args)

    def move(x, pairs):
        return lax.ppermute(x, "body", pairs)

    z_pairs = [[(i, (i + 4 * d) % count) for i in range(count)] for d in range(lines)]
    y_pairs = [(i, i ^ 2) for i in range(count)]
    c_pairs = [(i, i ^ 1) for i in range(count)]
    order = sorted(range(1, lines), key=lambda d: min(d, lines - d))
    places = [4 * d + j for d in order[::-1] + [0] for j in range(4)]
    for step in range(ITERS):
        blocks = [None] * count
        own = sources if step else same
        blocks[0] = sources
        for d in order:
            blocks[4 * d] = move(own if d == order[-1] else sources, z_pairs[d])
        far = order[-1]
        blocks[2] = move(sources, y_pairs)
        if not step:
            cross_b = split_late(all_blocks, same)
            ends = [4 * order[0], 4 * order[-2]]
            blocks[ends[0]], blocks[ends[1]] = after(*[blocks[e] for e in ends], cross_b)
        blocks[4 * far + 2] = move(own, [(i, j ^ 2) for i, j in z_pairs[far]])
        for d in order[:-1]:
            blocks[4 * d + 2] = move(blocks[4 * d], y_pairs)
        passed = [blocks[4 * d + 2] for d in order[:-1]]
        pair = after(blocks[4 * far], blocks[4 * far + 2], *passed)
        blocks[4 * far], blocks[4 * far + 2] = pair
        for d in [0] + order:
            blocks[4 * d + 1] = move(blocks[4 * d], c_pairs)
            blocks[4 * d + 3] = move(blocks[4 * d + 2], c_pairs)
        args = (neighbours, *[blocks[j] for j in places], field, cross_a, cross_b, inverse)
        if step == ITERS - 1:
            sources, part = sweep(True, *args, panel_weight)
        else:
            sources = sweep(False, *args)
    lines_sum = []
    for flip in (0, 2):
        terms = []
        for d in range(lines):
            pairs = [(i, j ^ flip) for i, j in z_pairs[d]]
            terms.append(move(part, pairs) if d or flip else part)
        while len(terms) > 1:
            half = len(terms) // 2
            terms = [terms[i] + terms[i + half] for i in range(half)]
        lines_sum.append(terms[0])
    part = lines_sum[0] + lines_sum[1]
    part = part + move(part, c_pairs)
    return (sources.reshape(1, 2, heads, panels), part[None])


def solution(mesh):
    return jax.shard_map(
        functools.partial(body, mesh.shape["body"]),
        mesh=mesh,
        in_specs=(
            P(("farm", "body"), None, None, None),
            P(("farm", "body"), None, None, None),
            P(("farm", "body"), None, None, None, None),
            P(("farm", "body"), None),
            P(("farm", "body"), None),
        ),
        out_specs=(P(("farm", "body"), None, None, None), P("farm", None, None)),
        check_vma=False,
    )
```

```python
import functools

import jax
import jax.numpy as jnp
from jax import lax
from jax.experimental import pallas as pl
from jax.experimental.pallas import tpu as pltpu
from jax.sharding import PartitionSpec as P

ITERS = 6
NT = (((1,), (1,)), ((), ()))
LIMIT = 14 * 2**20
VMEM = pl.BlockSpec(memory_space=pltpu.VMEM)
SMEM = pl.BlockSpec(memory_space=pltpu.SMEM)
HBM = pl.BlockSpec(memory_space=pltpu.HBM)


def split(x):
    hi = x.astype(jnp.bfloat16)
    lo = (x - hi.astype(jnp.float32)).astype(jnp.bfloat16)
    return hi, lo


def turn(x, heads):
    return jnp.concatenate([-x[heads:], x[:heads]], axis=0)


def split_all(src, wide, buffers, sems, base=0):
    _, rows, cols = src.shape
    count = 2 * wide.shape[1] // cols
    depth, chunk, _ = buffers.shape
    steps = [(j, r) for j in range(count) for r in range(0, rows, chunk)]

    def copy(i):
        j, r = steps[i]
        return pltpu.make_async_copy(
            src.at[base + j, pl.ds(r, chunk)], buffers.at[i % depth], sems.at[i % depth]
        )

    for i in range(min(depth, len(steps))):
        copy(i).start()
    for i, (j, r) in enumerate(steps):
        copy(i).wait()
        hi, lo = split(buffers[i % depth])
        slot, c = j // 2, j % 2
        at = 2 * c * rows + r
        wide[at:at + chunk, slot * cols:(slot + 1) * cols] = hi
        wide[at + rows:at + rows + chunk, slot * cols:(slot + 1) * cols] = lo
        if i + depth < len(steps):
            copy(i + depth).start()


def put_field(lhs, slot, x):
    rows, panels = x.shape
    hi, lo = split(x)
    lhs[:rows, slot * panels:(slot + 1) * panels] = hi
    lhs[rows:, slot * panels:(slot + 1) * panels] = lo


def product(lhs, wides, heads):
    panels = wides[0].shape[0] // 4
    rows = 2 * heads

    def real(c):
        total = None
        for part in range(2):
            row, at = (2 * c + part) * panels, 0
            for wide in wides:
                width = wide.shape[1]
                term = lax.dot_general(
                    wide[row:row + panels, :], lhs[:, at:at + width], NT,
                    preferred_element_type=jnp.float32,
                )
                total = term if total is None else total + term
                at += width
        flat = total.T
        return flat[:rows] + flat[rows:]

    return real(0) + turn(real(1), heads)


def first_kernel(heads, inverse, field_ref, wide, out_ref, lhs, buffers, sems):
    split_all(inverse, wide, buffers, sems)
    put_field(lhs, 0, field_ref[...])
    out_ref[...] = product(lhs, [wide], heads)


def near_kernel(src, field_ref, wide, same_ref, buffers, sems):
    split_all(src, wide, buffers, sems)
    same_ref[...] = field_ref[...]


def late_kernel(base, src, waited, wide, buffers, sems):
    del waited
    split_all(src, wide, buffers, sems, base)


def after_kernel(*refs):
    del refs


def after(a, b, *others):
    here = pl.BlockSpec(memory_space=pl.ANY)
    like = jax.ShapeDtypeStruct(a.shape, a.dtype)
    return pl.pallas_call(
        after_kernel,
        in_specs=[here] * (2 + len(others)),
        out_specs=[here] * 2,
        out_shape=[like] * 2,
        input_output_aliases={0: 0, 1: 1},
        compiler_params=pltpu.CompilerParams(vmem_limit_bytes=2**20),
    )(a, b, *others)


def sweep_kernel(heads, slots, places, last, row_ref, *refs):
    count = len(places)
    blocks = dict(zip(places, refs[:count]))
    field_ref, cross_a, cross_b, inverse = refs[count:count + 4]
    refs = refs[count + 4:]
    if last:
        weight_ref, out_ref, part_ref, near, lhs, short = refs
    else:
        out_ref, near, lhs, short = refs
    me = lax.axis_index("body")
    lines = count // 4
    for k in range(slots):
        index = row_ref[0, k]
        dz = lax.rem(me // 4 + lines - index // 4, lines)
        at = dz * 4 + jnp.bitwise_xor(lax.rem(index, 4), lax.rem(me, 4))
        at = jnp.where(index < 0, -1, at)
        for j in range(count):
            @pl.when(at == j)
            def _():
                near[...] = blocks[j][...]

        @pl.when(index < 0)
        def _():
            near[...] = jnp.zeros_like(near)

        put_field(lhs, k, near[...])

    put_field(short, 0, field_ref[...] - product(lhs, [cross_a, cross_b], heads))
    value = product(short, [inverse], heads)
    out_ref[...] = value
    if last:
        for c in range(2):
            part_ref[c:c + 1, :] = lax.dot_general(
                weight_ref[...], value[c * heads:(c + 1) * heads], NT,
                precision=lax.Precision.HIGHEST, preferred_element_type=jnp.float32,
            )


def body(count, incident, self_inverse, cross_blocks, neighbours, panel_weight):
    _, _, heads, panels = incident.shape
    slots = cross_blocks.shape[1]
    rows = 2 * heads
    field = incident.reshape(rows, panels)
    lines = count // 4
    out = jax.ShapeDtypeStruct((rows, panels), jnp.float32)
    tiny = jax.ShapeDtypeStruct((2, heads), jnp.float32)
    params = pltpu.CompilerParams(vmem_limit_bytes=LIMIT)
    chunk = panels // 2
    inverse, sources = pl.pallas_call(
        functools.partial(first_kernel, heads),
        in_specs=[HBM, VMEM],
        out_specs=[VMEM, VMEM],
        out_shape=[jax.ShapeDtypeStruct((4 * panels, panels), jnp.bfloat16), out],
        scratch_shapes=[
            pltpu.VMEM((2 * rows, panels), jnp.bfloat16),
            pltpu.VMEM((4, chunk, panels), jnp.float32),
            pltpu.SemaphoreType.DMA((4,)),
        ],
        compiler_params=params,
    )(pltpu.with_memory_space_constraint(self_inverse[0], pltpu.HBM), field)
    early = slots // 2
    all_blocks = pltpu.with_memory_space_constraint(
        cross_blocks[0].reshape(2 * slots, panels, panels), pltpu.HBM
    )
    scratch = [pltpu.VMEM((6, chunk, panels), jnp.float32), pltpu.SemaphoreType.DMA((6,))]

    def cost(count):
        size = count * 8 * panels * panels
        return pl.CostEstimate(flops=4 * size, bytes_accessed=size, transcendentals=0)

    cross_a, same = pl.pallas_call(
        near_kernel,
        in_specs=[HBM, VMEM],
        out_specs=[VMEM, VMEM],
        out_shape=[jax.ShapeDtypeStruct((4 * panels, early * panels), jnp.bfloat16), out],
        scratch_shapes=scratch,
        compiler_params=params,
        cost_estimate=cost(early),
    )(all_blocks, sources)
    split_late = pl.pallas_call(
        functools.partial(late_kernel, 2 * early),
        in_specs=[HBM, pl.BlockSpec(memory_space=pl.ANY)],
        out_specs=VMEM,
        out_shape=jax.ShapeDtypeStruct((4 * panels, (slots - early) * panels), jnp.bfloat16),
        scratch_shapes=scratch,
        compiler_params=params,
        cost_estimate=cost(slots - early),
    )

    def sweep(last, *args):
        return pl.pallas_call(
            functools.partial(sweep_kernel, heads, slots, places, last),
            in_specs=[SMEM] + [VMEM] * (len(args) - 1),
            out_specs=[VMEM, VMEM] if last else VMEM,
            out_shape=[out, tiny] if last else out,
            scratch_shapes=[
                pltpu.VMEM((rows, panels), jnp.float32),
                pltpu.VMEM((2 * rows, slots * panels), jnp.bfloat16),
                pltpu.VMEM((2 * rows, panels), jnp.bfloat16),
            ],
            compiler_params=params,
        )(*args)

    def move(x, pairs):
        return lax.ppermute(x, "body", pairs)

    z_pairs = [[(i, (i + 4 * d) % count) for i in range(count)] for d in range(lines)]
    y_pairs = [(i, i ^ 2) for i in range(count)]
    c_pairs = [(i, i ^ 1) for i in range(count)]
    order = sorted(range(1, lines), key=lambda d: min(d, lines - d))
    places = [4 * d + j for d in order[::-1] + [0] for j in range(4)]
    for step in range(ITERS):
        blocks = [None] * count
        own = sources if step else same
        blocks[0] = sources
        for d in order:
            blocks[4 * d] = move(own if d == order[-1] else sources, z_pairs[d])
        far = order[-1]
        blocks[2] = move(sources, y_pairs)
        if not step:
            cross_b = split_late(all_blocks, same)
            ends = [4 * order[0], 4 * order[-2]]
            blocks[ends[0]], blocks[ends[1]] = after(*[blocks[e] for e in ends], cross_b)
        blocks[4 * far + 2] = move(own, [(i, j ^ 2) for i, j in z_pairs[far]])
        for d in order[:-1]:
            blocks[4 * d + 2] = move(blocks[4 * d], y_pairs)
        for d in [0] + order[:-1]:
            blocks[4 * d + 1] = move(blocks[4 * d], c_pairs)
            blocks[4 * d + 3] = move(blocks[4 * d + 2], c_pairs)
        passed = [blocks[4 * d + 2] for d in order[:-1]] + [blocks[1], blocks[3]]
        pair = after(blocks[4 * far], blocks[4 * far + 2], *passed)
        blocks[4 * far], blocks[4 * far + 2] = pair
        blocks[4 * far + 1] = move(blocks[4 * far], c_pairs)
        blocks[4 * far + 3] = move(blocks[4 * far + 2], c_pairs)
        args = (neighbours, *[blocks[j] for j in places], field, cross_a, cross_b, inverse)
        if step == ITERS - 1:
            sources, part = sweep(True, *args, panel_weight)
        else:
            sources = sweep(False, *args)
    terms = [part] + [move(part, z_pairs[d]) for d in range(1, lines)]
    while len(terms) > 1:
        half = len(terms) // 2
        terms = [terms[i] + terms[i + half] for i in range(half)]
    part = terms[0]
    part = part + move(part, y_pairs)
    part = part + move(part, c_pairs)
    return (sources.reshape(1, 2, heads, panels), part[None])


def solution(mesh):
    return jax.shard_map(
        functools.partial(body, mesh.shape["body"]),
        mesh=mesh,
        in_specs=(
            P(("farm", "body"), None, None, None),
            P(("farm", "body"), None, None, None),
            P(("farm", "body"), None, None, None, None),
            P(("farm", "body"), None),
            P(("farm", "body"), None),
        ),
        out_specs=(P(("farm", "body"), None, None, None), P("farm", None, None)),
        check_vma=False,
    )
```
